256 devices in a mesh: pair: 8 (over y, z_hi), pw: 32 (over x, z_lo, core).
Axes of the slice: x: 4, y: 4, z: 8 (z_hi: 2, z_lo: 4; z = z_hi * 4 + z_lo), core: 2. Of those that a mesh axis runs over, the one named last changes fastest.
Arguments:
- pair_elements: bfloat16 [32768, 32768], P('pair', 'pw'), may hold values from -6 to 6
- subspace: bfloat16 [32768, 512], P('pw'), may hold values from -0.03125 to 0.03125
- val_energy: float32 [16], replicated, may hold values from -10 to -1
- cond_energy: float32 [2048], replicated, may hold values from 0.5 to 12
- val_index: int32 [32768], P('pair'), may hold values from 0 to 15, as said below
- cond_index: int32 [32768], P('pair'), may hold values from 0 to 2047, as said below
- frequencies: float32 [32], P('pw'), may hold values from 0.1 to 30
Outputs:
- chi: float32 [32, 512, 512], P('pw', 'pair')
The draws below stay inside these ranges and needn't reach their ends.
Inputs may be any that keep to these rules, and one draw needn't show every extreme that they name: `val_index`: every combination of a valence band and a conduction band is named by exactly one pair. `cond_index`: every combination of a valence band and a conduction band is named by exactly one pair.
All inputs are finite; a program needn't handle non-finite values.
Results may differ from the reference program's by a relative error of at most 0.00067.
Values may be sent and summed in bfloat16 or wider, within the bound.
No kernel may reach another device: no remote copies, remote signals or barrier semaphores. Data moves between devices by JAX's collectives and lax.ppermute only.
A program may use at most 64 MiB of HBM per device.

```python
import math
import jax
import jax.numpy as jnp
from jax import lax

PW = 32768
S = 512
F = 32
NV = 16
PAIRS = 32768
NC = 2048


def pair_table(key):
    mixed = jax.random.fold_in(key, 7)
    return jax.random.permutation(mixed, PAIRS).astype(jnp.int32)


def draw_val_index(key, part):
    return (pair_table(key) // NC).astype(jnp.int32)


def draw_cond_index(key, part):
    return (pair_table(key) % NC).astype(jnp.int32)


def block_scale(key, dims, shards, low, high):
    def one(position, shards_of):
        draws = jax.random.uniform(jax.random.fold_in(jax.random.fold_in(key, 6), position), (shards_of,), jnp.float32, low / len(shards), high / len(shards))
        return jnp.repeat(jnp.exp(draws), dims[position] // shards_of).reshape((-1,) + (1,) * (len(dims) - position - 1))

    level = one(*shards[0])
    for cut in shards[1:]:
        level = level * one(*cut)
    return level


def scatter_about(stream_key, shape, scale, bound, shards=(), held_as=jnp.bfloat16):
    entries = jax.random.normal(stream_key, shape, jnp.float32) * scale
    if len(shards) > 0:
        entries = block_scale(stream_key, shape, shards, -0.22, 0.18) * entries
    return jnp.clip(entries, min=-bound, max=bound).astype(held_as)


def setup_inputs(seed: int = 0) -> dict:
    arg_keys = jax.random.split(jax.random.key(seed), 8)
    return {
        "pair_elements": scatter_about(arg_keys[0], (PAIRS, PW), 1.0, 6.0, ((0, 8), (1, 32))),
        "subspace": scatter_about(arg_keys[1], (PW, S), PW ** -0.5, 0.03125, ((0, 32),)),
        "val_energy": jnp.clip(jax.random.uniform(arg_keys[2], (NV,), jnp.float32, -10.0, -1.0), -10.0, -1.0),
        "cond_energy": jnp.clip(jax.random.uniform(arg_keys[3], (NC,), jnp.float32, 0.5, 12.0), 0.5, 12.0),
        "val_index": draw_val_index(jax.random.fold_in(arg_keys[7], 71), 0),
        "cond_index": draw_cond_index(jax.random.fold_in(arg_keys[7], 71), 0),
        "frequencies": jnp.clip(jnp.exp(math.log(30.0) - 5.7037825 * jax.random.uniform(arg_keys[6], (F,), jnp.float32) ** block_scale(arg_keys[6], (F,), ((0, 32),), -0.2, 0.2)), 0.1, 30.0),
    }


def reference(pair_elements, subspace, val_energy, cond_energy, val_index, cond_index, frequencies):
    spacing = cond_energy[cond_index] - val_energy[val_index]
    weights = 2.0 * spacing[:, None] / (spacing[:, None] ** 2 + frequencies[None, :] ** 2)
    projected = jnp.dot(pair_elements, subspace, preferred_element_type=jnp.float32)
    coeffs = projected.astype(jnp.bfloat16)
    coeffs_wide = coeffs.astype(jnp.float32)

    def single_gram(column):
        weighted = (column[:, None] * coeffs_wide).astype(jnp.bfloat16)
        return jnp.dot(weighted.T, coeffs, preferred_element_type=jnp.float32)

    gram = lax.map(single_gram, weights.T)
    return gram * (-4.0 / PAIRS)
```

```python
import jax
import jax.numpy as jnp
from jax import lax
from jax.experimental import pallas as pl
from jax.experimental.pallas import tpu as pltpu
from jax.sharding import Mesh
from jax.sharding import PartitionSpec as P

PW = ("pw_x", "pw_z", "pw_c")
F32, BF16, I16 = jnp.float32, jnp.bfloat16, jnp.int16
TAIL = 16
VMEM_LIMIT = 48 * 1024 * 1024


def xor_permute(value, axis, mask):
    count = lax.axis_size(axis)
    return lax.ppermute(value, axis, [(i, i ^ mask) for i in range(count)])


def call(body, outs, *args, cost=0, **kwargs):
    moved = sum(a.size * a.dtype.itemsize for a in args)
    return pl.pallas_call(
        body,
        out_shape=[jax.ShapeDtypeStruct(shape, dtype) for shape, dtype in outs],
        compiler_params=pltpu.CompilerParams(vmem_limit_bytes=VMEM_LIMIT),
        cost_estimate=pl.CostEstimate(flops=cost, bytes_accessed=moved, transcendentals=0),
        **kwargs,
    )(*args)


def project(ids, pair_elements, subspace):
    count, width = ids.shape[0], subspace.shape[1]
    depth = subspace.shape[0]

    def body(ids_ref, a_ref, b_ref, o_ref):
        o_ref[...] = jnp.dot(a_ref[...], b_ref[...], preferred_element_type=F32)

    return pl.pallas_call(
        body,
        out_shape=jax.ShapeDtypeStruct((count * 256, width), F32),
        grid_spec=pltpu.PrefetchScalarGridSpec(
            num_scalar_prefetch=1,
            grid=(count,),
            in_specs=[
                pl.BlockSpec((256, depth), lambda i, ids_ref: (ids_ref[i], 0)),
                pl.BlockSpec((depth, width), lambda i, ids_ref: (0, 0)),
            ],
            out_specs=pl.BlockSpec((256, width), lambda i, ids_ref: (i, 0)),
        ),
        compiler_params=pltpu.CompilerParams(vmem_limit_bytes=VMEM_LIMIT),
        cost_estimate=pl.CostEstimate(
            flops=2 * count * 256 * depth * width, bytes_accessed=count * 256 * (2 * depth + 4 * width), transcendentals=0
        ),
    )(ids, pair_elements, subspace)


def pack(ref, value):
    rows = value.shape[0]
    top = jnp.max(jnp.max(jnp.abs(value), axis=0, keepdims=True), axis=1, keepdims=True)
    exponent = jnp.clip(jnp.ceil(jnp.log2(jnp.maximum(top, 1e-30) * (1.0 / 32000.0))), -100.0, 100.0)
    scaled = value * jnp.exp2(-exponent)
    ref[:rows, :] = jnp.round(scaled).astype(jnp.int32).astype(I16)
    ref[rows:, :] = jnp.broadcast_to(exponent, (TAIL, value.shape[1])).astype(jnp.int32).astype(I16)


def unpack(ref):
    rows = ref.shape[0] - TAIL
    tail = ref[rows:, :].astype(jnp.int32).astype(F32)
    step = jnp.exp2(tail[0:1, 0:1])
    return ref[:rows, :].astype(jnp.int32).astype(F32) * step


def first_messages(own_ref, other_ref, a_ref, b_ref):
    half = own_ref.shape[0] // 2
    pack(a_ref, own_ref[:half, :] + other_ref[:half, :])
    pack(b_ref, own_ref[half:, :] + other_ref[half:, :])


def second_messages(own_ref, other_ref, a_in, b_in, kept_ref, a_ref, b_ref):
    rows = own_ref.shape[0] // 4
    for part, (came, out) in enumerate(((a_in, a_ref), (b_in, b_ref))):
        here = 2 * part * rows
        total = own_ref[here : here + 2 * rows, :] + other_ref[here : here + 2 * rows, :] + unpack(came)
        kept_ref[part * rows : (part + 1) * rows, :] = total[:rows, :]
        pack(out, total[rows:, :])


def third_messages(z_ref, kept_ref, a_in, b_in, own_ref, m1_ref, m2_ref, m3_ref, work_ref):
    half = kept_ref.shape[0] // 2
    quarter = half // 2
    work_ref[:half, :] = kept_ref[:half, :] + unpack(a_in)
    work_ref[half:, :] = kept_ref[half:, :] + unpack(b_in)
    z = z_ref[0]

    def rows_of(owner):
        return work_ref[pl.ds(pl.multiple_of(owner * quarter, quarter), quarter), :]

    own_ref[...] = rows_of(z)
    for mask, out in ((1, m1_ref), (2, m2_ref), (3, m3_ref)):
        pack(out, rows_of(lax.bitwise_xor(z, mask)))


def last_sum(own_ref, m1_in, m2_in, m3_in, out_ref):
    out_ref[...] = (own_ref[...] + unpack(m1_in) + unpack(m2_in) + unpack(m3_in)).astype(BF16)


def weights_of(cond_index, val_index, cond_energy, val_energy, frequencies):
    shape = cond_index.shape

    def body(val_table, freq_ref, ci_ref, vi_ref, ce_ref, out_ref):
        index = ci_ref[...]
        high, low = index // 128, index % 128
        cond = jnp.zeros(shape, F32)
        for row in range(ce_ref.shape[0]):
            table = jnp.broadcast_to(ce_ref[row : row + 1, :], shape)
            cond = jnp.where(high == row, jnp.take_along_axis(table, low, axis=1), cond)
        level = vi_ref[...]
        val = jnp.zeros(shape, F32)
        for row in range(val_table.shape[0]):
            val = jnp.where(level == row, val_table[row], val)
        spacing = cond - val
        freq = freq_ref[0]
        out_ref[...] = 2.0 * spacing / (spacing * spacing + freq * freq)

    smem, vmem = pl.BlockSpec(memory_space=pltpu.SMEM), pl.BlockSpec(memory_space=pltpu.VMEM)
    return call(
        body,
        [(shape, F32)],
        val_energy,
        frequencies,
        cond_index,
        val_index,
        cond_energy,
        in_specs=[smem, smem, vmem, vmem, vmem],
        out_specs=[vmem],
    )[0]


def gram_step(blocks, weights, pieces, gram):
    width = pieces[0].shape[1]
    count = len(pieces)

    def body(blocks_ref, w_ref, *refs):
        came, out_ref = refs[:count], refs[-1]
        total = refs[count][...] if gram is not None else None
        for i, ref in enumerate(came):
            per = ref.shape[0] // 128
            parts = []
            for j in range(per):
                rows = ref[128 * j : 128 * (j + 1), :].astype(F32).T
                w = w_ref[pl.ds(blocks_ref[i * per + j], 1), :]
                parts.append((rows * w).astype(BF16))
            term = jnp.dot(jnp.concatenate(parts, axis=1), ref[...], preferred_element_type=F32)
            total = term if total is None else total + term
        out_ref[...] = total

    extra = [] if gram is None else [gram]
    smem, vmem = pl.BlockSpec(memory_space=pltpu.SMEM), pl.BlockSpec(memory_space=pltpu.VMEM)
    return call(
        body,
        [((width, width), F32)],
        blocks,
        weights,
        *pieces,
        *extra,
        cost=2 * width * width * sum(p.shape[0] for p in pieces),
        in_specs=[smem] + [vmem] * (1 + count + len(extra)),
        out_specs=[vmem],
    )[0]


def on_device(pair_elements, subspace, val_energy, cond_energy, val_index, cond_index, frequencies):
    x, z, core = (lax.axis_index(name).astype(jnp.int32) for name in PW)
    rows, width = pair_elements.shape[0], subspace.shape[1]
    eighth = rows // 8

    def block(owner, part):
        return 2 * (x ^ owner) + part

    sent = jnp.stack([block(1, 0), block(2, 0), block(3, 1), block(2, 1)])
    kept = jnp.stack([block(0, 0), block(3, 0), block(0, 1), block(1, 1)])
    mine, theirs = 8 * core, 8 * (1 - core)
    sent_other = project(sent + theirs, pair_elements, subspace)
    sent_in = xor_permute(sent_other, "pw_c", 1)
    sent_own = project(sent + mine, pair_elements, subspace)
    kept_other = project(kept + theirs, pair_elements, subspace)
    kept_in = xor_permute(kept_other, "pw_c", 1)
    message = lambda count: ((count + TAIL, width), I16)
    a, b = call(first_messages, [message(eighth)] * 2, sent_own, sent_in)
    a, b = xor_permute(a, "pw_x", 1), xor_permute(b, "pw_x", 3)
    kept_own = project(kept + mine, pair_elements, subspace)
    weights = weights_of(
        cond_index.reshape(-1, 128), val_index.reshape(-1, 128), cond_energy.reshape(-1, 128), val_energy, frequencies
    )
    held, a, b = call(
        second_messages, [((eighth, width), F32)] + [message(eighth // 2)] * 2, kept_own, kept_in, a, b
    )
    a, b = xor_permute(a, "pw_x", 3), xor_permute(b, "pw_x", 1)
    smem, vmem = pl.BlockSpec(memory_space=pltpu.SMEM), pl.BlockSpec(memory_space=pltpu.VMEM)
    piece = eighth // 4
    own, *out = call(
        third_messages,
        [((piece, width), F32)] + [message(piece)] * 3,
        z[None],
        held,
        a,
        b,
        in_specs=[smem] + [vmem] * 3,
        out_specs=[vmem] * 4,
        scratch_shapes=[pltpu.VMEM((eighth, width), F32)],
    )
    came = [xor_permute(value, "pw_z", mask + 1) for mask, value in enumerate(out)]
    coeffs = call(last_sum, [((piece, width), BF16)], own, *came)[0]

    quarter = jnp.concatenate([coeffs] + [xor_permute(coeffs, "pw_z", mask) for mask in (1, 2, 3)], axis=0)
    by_owner = [quarter] + [xor_permute(quarter, "pw_x", mask) for mask in (1, 3, 2)]
    by_core = [xor_permute(value, "pw_c", 1) for value in by_owner]
    place = jnp.stack([z ^ mask for mask in range(4)])

    def places(masks):
        return jnp.concatenate([16 * k + 4 * (x ^ mask) + place for mask in masks for k in (core, 1 - core)])

    gram = gram_step(places((0,)), weights, [by_owner[0], by_core[0]], None)
    gram = gram_step(places((1, 3)), weights, [by_owner[1], by_core[1], by_owner[2], by_core[2]], gram)
    gram = gram_step(places((2,)), weights, [by_owner[3], by_core[3]], gram)
    groups = lax.axis_size("pair")
    pieces = lax.all_to_all(gram.reshape(groups, -1, width), "pair", 0, 0, tiled=True)
    factor = -4.0 / (rows * groups)
    return (jnp.sum(pieces, axis=0) * factor)[None]


def solution(mesh):
    torus = Mesh(mesh.devices.reshape(mesh.shape["pair"], 4, 4, 2), ("pair",) + PW)
    return jax.shard_map(
        on_device,
        mesh=torus,
        in_specs=(P("pair", PW), P(PW, None), P(), P(), P("pair"), P("pair"), P(PW)),
        out_specs=P(PW, "pair", None),
        check_vma=False,
    )
```

```python
import jax
import jax.numpy as jnp
from jax import lax
from jax.experimental import pallas as pl
from jax.experimental.pallas import tpu as pltpu
from jax.sharding import Mesh
from jax.sharding import PartitionSpec as P

PW = ("pw_x", "pw_z", "pw_c")
F32, BF16, I16 = jnp.float32, jnp.bfloat16, jnp.int16
TAIL = 16
VMEM_LIMIT, VMEM_FULL = 48 * 1024 * 1024, 63 * 1024 * 1024
SMEM, VMEM = pl.BlockSpec(memory_space=pltpu.SMEM), pl.BlockSpec(memory_space=pltpu.VMEM)


def xor_permute(value, axis, mask):
    count = lax.axis_size(axis)
    return lax.ppermute(value, axis, [(i, i ^ mask) for i in range(count)])


def call(body, outs, *args, cost=0, **kwargs):
    moved = sum(a.size * a.dtype.itemsize for a in args)
    return pl.pallas_call(
        body,
        out_shape=[jax.ShapeDtypeStruct(shape, dtype) for shape, dtype in outs],
        compiler_params=pltpu.CompilerParams(vmem_limit_bytes=VMEM_LIMIT),
        cost_estimate=pl.CostEstimate(flops=cost, bytes_accessed=moved, transcendentals=0),
        **kwargs,
    )(*args)


def project(ids, pair_elements, subspace, fetch, outs):
    count, (depth, width) = ids.shape[0], subspace.shape
    per = count // outs

    def body(ids_ref, a_ref, b_ref, *refs):
        out_refs, (held, sems), (b_held,) = refs[:outs], refs[outs : outs + 2], refs[outs + 2 :] or (b_ref,)
        copies = []
        if fetch:
            copies.append(pltpu.make_async_copy(b_ref, b_held, sems.at[count]))
        for i in range(count):
            block = a_ref.at[pl.ds(pl.multiple_of(ids_ref[i] * 256, 256), 256), :]
            copies.append(pltpu.make_async_copy(block, held.at[pl.ds(256 * i, 256), :], sems.at[i]))
        for copy in copies:
            copy.start()
        if fetch:
            copies.pop(0).wait()
        for o, out_ref in enumerate(out_refs):
            for copy in copies[o * per : (o + 1) * per]:
                copy.wait()
            rows = held[o * per * 256 : (o + 1) * per * 256, :]
            out_ref[...] = jnp.dot(rows, b_held[...], preferred_element_type=F32)

    return pl.pallas_call(
        body,
        out_shape=[jax.ShapeDtypeStruct((per * 256, width), F32)] * outs,
        in_specs=[SMEM, pl.BlockSpec(memory_space=pl.ANY), pl.BlockSpec(memory_space=pl.ANY) if fetch else VMEM],
        out_specs=[VMEM] * outs,
        scratch_shapes=[pltpu.VMEM((count * 256, depth), BF16), pltpu.SemaphoreType.DMA((count + 1,))]
        + ([pltpu.VMEM((depth, width), BF16)] if fetch else []),
        compiler_params=pltpu.CompilerParams(vmem_limit_bytes=VMEM_FULL if fetch else VMEM_LIMIT),
        cost_estimate=pl.CostEstimate(
            flops=2 * count * 256 * depth * width, bytes_accessed=count * 256 * (2 * depth + 4 * width), transcendentals=0
        ),
    )(ids, pair_elements, subspace)


def pack(ref, value):
    rows = value.shape[0]
    top = jnp.maximum(jnp.max(jnp.abs(value), axis=0, keepdims=True), 1e-30)
    level = jnp.clip(jnp.ceil(jnp.log2(top * (1.0 / 32000.0)) * 256.0), -32000.0, 32000.0)
    scaled = value * jnp.exp2(level * (-1.0 / 256.0))
    ref[:rows, :] = jnp.round(scaled).astype(jnp.int32).astype(I16)
    ref[rows:, :] = jnp.broadcast_to(level, (TAIL, value.shape[1])).astype(jnp.int32).astype(I16)


def unpack(ref):
    rows = ref.shape[0] - TAIL
    level = ref[rows:, :].astype(jnp.int32).astype(F32)[0:1, :]
    return ref[:rows, :].astype(jnp.int32).astype(F32) * jnp.exp2(level * (1.0 / 256.0))


def first_messages(own_ref, other_ref, a_ref, b_ref):
    half = own_ref.shape[0] // 2
    pack(a_ref, own_ref[:half, :] + other_ref[:half, :])
    pack(b_ref, own_ref[half:, :] + other_ref[half:, :])


def add(a_ref, b_ref, out_ref):
    out_ref[...] = a_ref[...] + b_ref[...]


def second_messages(sum_ref, a_in, b_in, kept_ref, a_ref, b_ref):
    rows = sum_ref.shape[0] // 4
    for part, (came, out) in enumerate(((a_in, a_ref), (b_in, b_ref))):
        here = 2 * part * rows
        total = sum_ref[here : here + 2 * rows, :] + unpack(came)
        kept_ref[part * rows : (part + 1) * rows, :] = total[:rows, :]
        pack(out, total[rows:, :])


def third_messages(z_ref, kept_ref, a_in, b_in, own_ref, m1_ref, m2_ref, m3_ref, work_ref):
    half = kept_ref.shape[0] // 2
    work_ref[:half, :] = kept_ref[:half, :] + unpack(a_in)
    work_ref[half:, :] = kept_ref[half:, :] + unpack(b_in)
    split_four(z_ref[0], work_ref, own_ref, (m1_ref, m2_ref, m3_ref))


def split_four(here, work_ref, own_ref, message_refs):
    quarter = work_ref.shape[0] // 4

    def rows_of(owner):
        return work_ref[pl.ds(pl.multiple_of(owner * quarter, quarter), quarter), :]

    own_ref[...] = rows_of(here)
    for mask, out in enumerate(message_refs):
        pack(out, rows_of(lax.bitwise_xor(here, mask + 1)))


def last_sum(own_ref, m1_in, m2_in, m3_in, out_ref):
    out_ref[...] = (own_ref[...] + unpack(m1_in) + unpack(m2_in) + unpack(m3_in)).astype(BF16)


def gram_messages(y_ref, mine_ref, came_ref, own_ref, m1_ref, m2_ref, m3_ref, work_ref):
    work_ref[...] = mine_ref[...] + came_ref[...]
    split_four(y_ref[0], work_ref, own_ref, (m1_ref, m2_ref, m3_ref))


def gram_halves(half_ref, own_ref, m1_in, m2_in, m3_in, kept_ref, out_ref, work_ref):
    rows = kept_ref.shape[0]
    work_ref[...] = own_ref[...] + unpack(m1_in) + unpack(m2_in) + unpack(m3_in)
    here = half_ref[0]
    kept_ref[...] = work_ref[pl.ds(pl.multiple_of(here * rows, rows), rows), :]
    pack(out_ref, work_ref[pl.ds(pl.multiple_of((1 - here) * rows, rows), rows), :])


def weights_of(cond_index, val_index, cond_energy, val_energy, *frequencies):
    shape, count = cond_index.shape, len(frequencies)

    def body(val_table, *refs):
        freq_refs, (ci_ref, vi_ref, ce_ref), out_refs = refs[:count], refs[count : count + 3], refs[count + 3 :]
        index = ci_ref[...]
        high, low = index // 128, index % 128
        cond = jnp.zeros(shape, F32)
        for row in range(ce_ref.shape[0]):
            table = jnp.broadcast_to(ce_ref[row : row + 1, :], shape)
            cond = jnp.where(high == row, jnp.take_along_axis(table, low, axis=1), cond)
        level = vi_ref[...]
        val = jnp.zeros(shape, F32)
        for row in range(val_table.shape[0]):
            val = jnp.where(level == row, val_table[row], val)
        spacing = cond - val
        for freq_ref, out_ref in zip(freq_refs, out_refs):
            freq = freq_ref[0]
            out_ref[...] = 2.0 * spacing / (spacing * spacing + freq * freq)

    return call(
        body,
        [(shape, F32)] * count,
        val_energy,
        *frequencies,
        cond_index,
        val_index,
        cond_energy,
        in_specs=[SMEM] * (1 + count) + [VMEM] * 3,
        out_specs=[VMEM] * count,
    )


def gram_step(blocks, weights, pieces, grams):
    width = pieces[0].shape[1]
    count, kinds = len(pieces), len(weights)

    def body(blocks_ref, *refs):
        w_refs, came, before, out_refs = refs[:kinds], refs[kinds : kinds + count], refs[kinds + count : -kinds], refs[-kinds:]
        totals = [ref[...] for ref in before] or [None] * kinds
        place = 0
        for ref in came:
            parts = [[] for _ in range(kinds)]
            for j in range(ref.shape[0] // 128):
                rows = ref[128 * j : 128 * (j + 1), :].astype(F32).T
                for part, w_ref in zip(parts, w_refs):
                    part.append((rows * w_ref[pl.ds(blocks_ref[place], 1), :]).astype(BF16))
                place += 1
            for kind, part in enumerate(parts):
                term = jnp.dot(jnp.concatenate(part, axis=1), ref[...], preferred_element_type=F32)
                totals[kind] = term if totals[kind] is None else totals[kind] + term
        for out_ref, total in zip(out_refs, totals):
            out_ref[...] = total

    return call(
        body,
        [((width, width), F32)] * kinds,
        blocks,
        *weights,
        *pieces,
        *grams,
        cost=2 * kinds * width * width * sum(p.shape[0] for p in pieces),
        in_specs=[SMEM] + [VMEM] * (kinds + count + len(grams)),
        out_specs=[VMEM] * kinds,
    )


def on_device(pair_elements, subspace, val_energy, cond_energy, val_index, cond_index, frequencies):
    x, z, core = (lax.axis_index(name).astype(jnp.int32) for name in PW)
    pair = lax.axis_index("pair").astype(jnp.int32)
    rows, width = pair_elements.shape[0], subspace.shape[1]
    eighth = rows // 8
    message = lambda count: ((count + TAIL, width), I16)
    sums = lambda count: ((count, width), F32)

    def block(owner, part):
        return 2 * (x ^ owner) + part

    sent = jnp.stack([block(1, 0), block(2, 0), block(3, 1), block(2, 1)])
    kept = jnp.stack([block(0, 0), block(3, 0), block(0, 1), block(1, 1)])
    mine, theirs = 8 * core, 8 * (1 - core)
    (sent_other,) = project(sent + theirs, pair_elements, subspace, True, 1)
    sent_in = xor_permute(sent_other, "pw_c", 1)
    sent_own, kept_other = project(jnp.concatenate([sent + mine, kept + theirs]), pair_elements, subspace, True, 2)
    kept_in = xor_permute(kept_other, "pw_c", 1)
    a, b = call(first_messages, [message(eighth)] * 2, sent_own, sent_in)
    kept_ids, a, b = lax.optimization_barrier((kept + mine, a, b))
    a, b = xor_permute(a, "pw_x", 1), xor_permute(b, "pw_x", 3)
    (kept_own,) = project(kept_ids, pair_elements, subspace, False, 1)
    kept_sum = call(add, [sums(2 * eighth)], kept_own, kept_in)[0]
    weights = weights_of(
        cond_index.reshape(-1, 128),
        val_index.reshape(-1, 128),
        cond_energy.reshape(-1, 128),
        val_energy,
        frequencies,
        xor_permute(frequencies, "pw_c", 1),
    )
    kept_sum, weights = lax.optimization_barrier((kept_sum, weights))
    held, a, b = call(second_messages, [sums(eighth)] + [message(eighth // 2)] * 2, kept_sum, a, b)
    a, b = xor_permute(a, "pw_x", 3), xor_permute(b, "pw_x", 1)
    piece = eighth // 4
    own, *out = call(
        third_messages,
        [sums(piece)] + [message(piece)] * 3,
        z[None],
        held,
        a,
        b,
        in_specs=[SMEM] + [VMEM] * 3,
        out_specs=[VMEM] * 4,
        scratch_shapes=[pltpu.VMEM((eighth, width), F32)],
    )
    came = [xor_permute(value, "pw_z", mask + 1) for mask, value in enumerate(out)]
    coeffs = call(last_sum, [((piece, width), BF16)], own, *came)[0]

    near, far, across = (xor_permute(coeffs, "pw_z", mask) for mask in (1, 2, 3))
    top, bottom = jnp.concatenate([coeffs, near], axis=0), jnp.concatenate([far, across], axis=0)
    place = jnp.stack([z ^ mask for mask in range(4)]) + 16 * core
    top1, top3 = xor_permute(top, "pw_x", 1), xor_permute(top, "pw_x", 3)
    bottom1, bottom3 = xor_permute(bottom, "pw_x", 1), xor_permute(bottom, "pw_x", 3)

    def places(*masks):
        return jnp.concatenate([4 * (x ^ mask) + place for mask in masks])

    grams = gram_step(places(0), weights, [top, bottom], [])
    bottom1, top3, grams = lax.optimization_barrier((bottom1, top3, grams))
    top2, bottom2 = xor_permute(top3, "pw_x", 1), xor_permute(bottom1, "pw_x", 3)
    grams = gram_step(places(1, 3), weights, [top1, bottom1, top3, bottom3], grams)
    mine, theirs = gram_step(places(2), weights, [top2, bottom2], grams)

    across = width // 4
    own, *out = call(
        gram_messages,
        [sums(across)] + [message(across)] * 3,
        (pair // 2)[None],
        mine,
        xor_permute(theirs, "pw_c", 1),
        in_specs=[SMEM] + [VMEM] * 2,
        out_specs=[VMEM] * 4,
        scratch_shapes=[pltpu.VMEM((width, width), F32)],
    )
    came = [xor_permute(value, "pair", 2 * (mask + 1)) for mask, value in enumerate(out)]
    own, out = call(
        gram_halves,
        [sums(across // 2), message(across // 2)],
        (pair % 2)[None],
        own,
        *came,
        in_specs=[SMEM] + [VMEM] * 4,
        out_specs=[VMEM] * 2,
        scratch_shapes=[pltpu.VMEM((across, width), F32)],
    )
    factor = -4.0 / (rows * lax.axis_size("pair"))

    def finish(own_ref, came_ref, out_ref):
        out_ref[...] = (own_ref[...] + unpack(came_ref)) * factor

    return call(finish, [sums(across // 2)], own, xor_permute(out, "pair", 1))[0][None]


def solution(mesh):
    torus = Mesh(mesh.devices.reshape(mesh.shape["pair"], 4, 4, 2), ("pair",) + PW)
    return jax.shard_map(
        on_device,
        mesh=torus,
        in_specs=(P("pair", PW), P(PW, None), P(), P(), P("pair"), P("pair"), P(PW)),
        out_specs=P(PW, "pair", None),
        check_vma=False,
    )
```

```python
import jax
import jax.numpy as jnp
from jax import lax
from jax.experimental import pallas as pl
from jax.experimental.pallas import tpu as pltpu
from jax.sharding import Mesh
from jax.sharding import PartitionSpec as P

PW = ("pw_x", "pw_z", "pw_c")
F32, BF16, I16 = jnp.float32, jnp.bfloat16, jnp.int16
TAIL = 16
STREAMS = 2
VMEM_LIMIT = 48 * 1024 * 1024
SMEM, VMEM = pl.BlockSpec(memory_space=pltpu.SMEM), pl.BlockSpec(memory_space=pltpu.VMEM)
ANY = pl.BlockSpec(memory_space=pl.ANY)


def xor_permute(value, axis, mask):
    count = lax.axis_size(axis)
    return lax.ppermute(value, axis, [(i, i ^ mask) for i in range(count)])


def call(body, outs, *args, specs=None, after=(), cost=0, scratch=()):
    specs = specs or [VMEM] * len(args)

    def kernel(*refs):
        body(*refs[: len(args)], *refs[len(args) + len(after) :])

    moved = sum(a.size * a.dtype.itemsize for a in args)
    return pl.pallas_call(
        kernel,
        out_shape=[jax.ShapeDtypeStruct(shape, dtype) for shape, dtype in outs],
        in_specs=specs + [VMEM] * len(after),
        out_specs=[VMEM] * len(outs),
        scratch_shapes=list(scratch),
        compiler_params=pltpu.CompilerParams(vmem_limit_bytes=VMEM_LIMIT),
        cost_estimate=pl.CostEstimate(flops=cost, bytes_accessed=moved, transcendentals=0),
    )(*args, *after)


def project(here, pair_elements, subspace, parts, after=()):
    depth, width = subspace.shape
    rows = pair_elements.shape[0] // (32 * STREAMS) * 2
    order = ((1, 0), (2, 0), (3, 1), (2, 1), (0, 0), (3, 0), (0, 1), (1, 1))
    per = len(order)

    def body(here_ref, a_ref, b_ref, *refs):
        out_refs, (held, sems) = refs[: len(parts)], refs[len(parts) :]
        x, core = here_ref[0], here_ref[2]
        copies = []
        for stream, own in parts:
            base = (core if own else 1 - core) * (16 // 2 * STREAMS) + stream * 2
            for owner, part in order:
                start = (base + lax.bitwise_xor(x, owner) * (2 * STREAMS) + part) * rows
                to = held.at[pl.ds(rows * len(copies), rows), :]
                copies.append(
                    pltpu.make_async_copy(a_ref.at[pl.ds(pl.multiple_of(start, rows), rows), :], to, sems.at[len(copies)])
                )
        for copy in copies:
            copy.start()
        for o, out_ref in enumerate(out_refs):
            for copy in copies[o * per : (o + 1) * per]:
                copy.wait()
            out_ref[...] = jnp.dot(held[o * per * rows : (o + 1) * per * rows, :], b_ref[...], preferred_element_type=F32)

    count = per * len(parts)
    return call(
        body,
        [((per * rows, width), F32)] * len(parts),
        here,
        pair_elements,
        subspace,
        specs=[SMEM, ANY, VMEM],
        after=after,
        cost=2 * count * rows * depth * width,
        scratch=[pltpu.VMEM((count * rows, depth), BF16), pltpu.SemaphoreType.DMA((count,))],
    )


def pack(ref, value):
    rows = value.shape[0]
    top = jnp.maximum(jnp.max(jnp.abs(value), axis=0, keepdims=True), 1e-30)
    level = jnp.clip(jnp.ceil(jnp.log2(top * (1.0 / 32000.0)) * 256.0), -32000.0, 32000.0)
    scaled = value * jnp.exp2(level * (-1.0 / 256.0))
    ref[:rows, :] = jnp.round(scaled).astype(jnp.int32).astype(I16)
    ref[rows:, :] = jnp.broadcast_to(level, (TAIL, value.shape[1])).astype(jnp.int32).astype(I16)


def unpack(ref):
    rows = ref.shape[0] - TAIL
    level = ref[rows:, :].astype(jnp.int32).astype(F32)[0:1, :]
    return ref[:rows, :].astype(jnp.int32).astype(F32) * jnp.exp2(level * (1.0 / 256.0))


def first_messages(own_ref, other_ref, kept_ref, a_ref, b_ref):
    rows = own_ref.shape[0] // 4
    pack(a_ref, own_ref[:rows, :] + other_ref[:rows, :])
    pack(b_ref, own_ref[rows : 2 * rows, :] + other_ref[rows : 2 * rows, :])
    kept_ref[...] = own_ref[2 * rows :, :] + other_ref[2 * rows :, :]


def second_messages(sum_ref, a_in, b_in, kept_ref, a_ref, b_ref):
    rows = sum_ref.shape[0] // 4
    for part, (came, out) in enumerate(((a_in, a_ref), (b_in, b_ref))):
        at = 2 * part * rows
        total = sum_ref[at : at + 2 * rows, :] + unpack(came)
        kept_ref[part * rows : (part + 1) * rows, :] = total[:rows, :]
        pack(out, total[rows:, :])


def split_four(mine, work_ref, own_ref, message_refs):
    quarter = work_ref.shape[0] // 4

    def rows_of(owner):
        return work_ref[pl.ds(pl.multiple_of(owner * quarter, quarter), quarter), :]

    own_ref[...] = rows_of(mine)
    for mask, out in enumerate(message_refs):
        pack(out, rows_of(lax.bitwise_xor(mine, mask + 1)))


def third_messages(here_ref, kept_ref, a_in, b_in, own_ref, m1_ref, m2_ref, m3_ref, work_ref):
    half = kept_ref.shape[0] // 2
    work_ref[:half, :] = kept_ref[:half, :] + unpack(a_in)
    work_ref[half:, :] = kept_ref[half:, :] + unpack(b_in)
    split_four(here_ref[1], work_ref, own_ref, (m1_ref, m2_ref, m3_ref))


def last_sum(own_ref, m1_in, m2_in, m3_in, out_ref):
    out_ref[...] = (own_ref[...] + unpack(m1_in) + unpack(m2_in) + unpack(m3_in)).astype(BF16)


def join(here_ref, p0_ref, p1_ref, p2_ref, p3_ref, out_ref):
    rows = p0_ref.shape[0]
    for mask, ref in enumerate((p0_ref, p1_ref, p2_ref, p3_ref)):
        owner = lax.bitwise_xor(here_ref[1], mask)
        out_ref[pl.ds(pl.multiple_of(owner * rows, rows), rows), :] = ref[...]


def gram_messages(here_ref, mine_ref, came_ref, own_ref, m1_ref, m2_ref, m3_ref, work_ref):
    work_ref[...] = mine_ref[...] + came_ref[...]
    split_four(here_ref[3] // 2, work_ref, own_ref, (m1_ref, m2_ref, m3_ref))


def gram_halves(here_ref, own_ref, m1_in, m2_in, m3_in, kept_ref, out_ref, work_ref):
    rows = kept_ref.shape[0]
    work_ref[...] = own_ref[...] + unpack(m1_in) + unpack(m2_in) + unpack(m3_in)
    half = here_ref[3] % 2
    kept_ref[...] = work_ref[pl.ds(pl.multiple_of(half * rows, rows), rows), :]
    pack(out_ref, work_ref[pl.ds(pl.multiple_of((1 - half) * rows, rows), rows), :])


def weights_of(cond_index, val_index, cond_energy, val_energy, frequencies, after):
    shape, count = cond_index.shape, len(frequencies)

    def body(val_table, *refs):
        freq_refs, (ci_ref, vi_ref, ce_ref), out_refs = refs[:count], refs[count : count + 3], refs[count + 3 :]
        index = ci_ref[...]
        high, low = index // 128, index % 128
        cond = jnp.zeros(shape, F32)
        for row in range(ce_ref.shape[0]):
            table = jnp.broadcast_to(ce_ref[row : row + 1, :], shape)
            cond = jnp.where(high == row, jnp.take_along_axis(table, low, axis=1), cond)
        level = vi_ref[...]
        val = jnp.zeros(shape, F32)
        for row in range(val_table.shape[0]):
            val = jnp.where(level == row, val_table[row], val)
        spacing = cond - val
        for freq_ref, out_ref in zip(freq_refs, out_refs):
            freq = freq_ref[0]
            out_ref[...] = 2.0 * spacing / (spacing * spacing + freq * freq)

    return call(
        body,
        [(shape, F32)] * count,
        val_energy,
        *frequencies,
        cond_index,
        val_index,
        cond_energy,
        specs=[SMEM] * (1 + count) + [VMEM] * 3,
        after=after,
    )


def gram_step(here, weights, pieces, places, grams, after=()):
    width = pieces[0].shape[1]
    count, kinds = len(pieces), len(weights)
    blocks = pieces[0].shape[0] // 128

    def body(here_ref, *refs):
        w_refs, came, before, out_refs = refs[:kinds], refs[kinds : kinds + count], refs[kinds + count : -kinds], refs[-kinds:]
        totals = [ref[...] for ref in before] or [None] * kinds
        for ref, (stream, owner) in zip(came, places):
            first = ((here_ref[2] * 4 + lax.bitwise_xor(here_ref[0], owner)) * STREAMS + stream) * blocks
            parts = [[] for _ in range(kinds)]
            for j in range(blocks):
                rows = ref[128 * j : 128 * (j + 1), :].astype(F32).T
                for part, w_ref in zip(parts, w_refs):
                    part.append((rows * w_ref[pl.ds(first + j, 1), :]).astype(BF16))
            for kind, part in enumerate(parts):
                term = jnp.dot(jnp.concatenate(part, axis=1), ref[...], preferred_element_type=F32)
                totals[kind] = term if totals[kind] is None else totals[kind] + term
        for out_ref, total in zip(out_refs, totals):
            out_ref[...] = total

    return call(
        body,
        [((width, width), F32)] * kinds,
        here,
        *weights,
        *pieces,
        *grams,
        cost=2 * kinds * width * width * sum(p.shape[0] for p in pieces),
        specs=[SMEM] + [VMEM] * (kinds + count + len(grams)),
        after=after,
    )


def on_device(pair_elements, subspace, val_energy, cond_energy, val_index, cond_index, frequencies):
    here = jnp.stack([lax.axis_index(name).astype(jnp.int32) for name in PW + ("pair",)])
    rows, width = pair_elements.shape[0], subspace.shape[1]
    unit = rows // (32 * STREAMS)
    message = lambda count: ((count + TAIL, width), I16)
    sums = lambda count: ((count, width), F32)
    both = range(STREAMS)

    (other,) = project(here, pair_elements, subspace, [(0, False)])
    came = [xor_permute(other, "pw_c", 1)]
    own, other = project(here, pair_elements, subspace, [(0, True), (1, False)], [other])
    came.append(xor_permute(other, "pw_c", 1))
    first = [message(4 * unit)] * 2
    kept, a, b = [None] * 2, [None] * 2, [None] * 2
    kept[0], a[0], b[0] = call(first_messages, [sums(8 * unit)] + first, own, came[0], after=[other])
    (own,) = project(here, pair_elements, subspace, [(1, True)], [kept[0]])
    kept[1], a[1], b[1] = call(first_messages, [sums(8 * unit)] + first, own, came[1])
    weights = weights_of(
        cond_index.reshape(-1, 128),
        val_index.reshape(-1, 128),
        cond_energy.reshape(-1, 128),
        val_energy,
        (frequencies, xor_permute(frequencies, "pw_c", 1)),
        [kept[1]],
    )

    last = weights[0]
    for s in both:
        a[s], b[s] = xor_permute(a[s], "pw_x", 1), xor_permute(b[s], "pw_x", 3)
    for s in both:
        last, a[s], b[s] = call(
            second_messages, [sums(4 * unit)] + [message(2 * unit)] * 2, kept[s], a[s], b[s], after=[last]
        )
        kept[s] = last
        a[s], b[s] = xor_permute(a[s], "pw_x", 3), xor_permute(b[s], "pw_x", 1)
    came = [None] * 2
    for s in both:
        last, *out = call(
            third_messages,
            [sums(unit)] + [message(unit)] * 3,
            here,
            kept[s],
            a[s],
            b[s],
            specs=[SMEM] + [VMEM] * 3,
            after=[last],
            scratch=[pltpu.VMEM((4 * unit, width), F32)],
        )
        came[s] = [last] + [xor_permute(value, "pw_z", mask + 1) for mask, value in enumerate(out)]

    pieces = [None] * 2
    for s in both:
        last = call(last_sum, [((unit, width), BF16)], *came[s], after=[last])[0]
        pieces[s] = [last] + [xor_permute(last, "pw_z", mask) for mask in (1, 2, 3)]
    quarters, near, far = [None] * 2, [None] * 2, [None] * 2
    for s in both:
        last = call(join, [((4 * unit, width), BF16)], here, *pieces[s], specs=[SMEM] + [VMEM] * 4, after=[last])[0]
        quarters[s] = last
        near[s], far[s] = xor_permute(last, "pw_x", 1), xor_permute(last, "pw_x", 3)
        near[s], far[s] = lax.optimization_barrier((near[s], far[s]))
    across = [xor_permute(far[0], "pw_x", 1), xor_permute(near[1], "pw_x", 3)]
    grams = gram_step(here, weights, quarters, [(0, 0), (1, 0)], [], [last])
    grams = gram_step(here, weights, [near[0], far[0]], [(0, 1), (0, 3)], grams)
    grams = gram_step(here, weights, [near[1], far[1], across[0]], [(1, 1), (1, 3), (0, 2)], grams)
    mine, theirs = gram_step(here, weights, [across[1]], [(1, 2)], grams)

    part = width // 4
    own, *out = call(
        gram_messages,
        [sums(part)] + [message(part)] * 3,
        here,
        mine,
        xor_permute(theirs, "pw_c", 1),
        specs=[SMEM] + [VMEM] * 2,
        scratch=[pltpu.VMEM((width, width), F32)],
    )
    came = [xor_permute(value, "pair", 2 * (mask + 1)) for mask, value in enumerate(out)]
    own, out = call(
        gram_halves,
        [sums(part // 2), message(part // 2)],
        here,
        own,
        *came,
        specs=[SMEM] + [VMEM] * 4,
        scratch=[pltpu.VMEM((part, width), F32)],
    )
    factor = -4.0 / (rows * lax.axis_size("pair"))

    def finish(own_ref, came_ref, out_ref):
        out_ref[...] = (own_ref[...] + unpack(came_ref)) * factor

    return call(finish, [sums(part // 2)], own, xor_permute(out, "pair", 1))[0][None]


def solution(mesh):
    torus = Mesh(mesh.devices.reshape(mesh.shape["pair"], 4, 4, 2), ("pair",) + PW)
    return jax.shard_map(
        on_device,
        mesh=torus,
        in_specs=(P("pair", PW), P(PW, None), P(), P(), P("pair"), P("pair"), P(PW)),
        out_specs=P(PW, "pair", None),
        check_vma=False,
    )
```

```python
import jax
import jax.numpy as jnp
from jax import lax
from jax.experimental import pallas as pl
from jax.experimental.pallas import tpu as pltpu
from jax.sharding import Mesh
from jax.sharding import PartitionSpec as P

PW = ("pw_x", "pw_z", "pw_c")
F32, BF16, I16 = jnp.float32, jnp.bfloat16, jnp.int16
TAIL = 16
VMEM_LIMIT = 48 * 1024 * 1024
SMEM, VMEM = pl.BlockSpec(memory_space=pltpu.SMEM), pl.BlockSpec(memory_space=pltpu.VMEM)
ANY = pl.BlockSpec(memory_space=pl.ANY)


def xor_permute(value, axis, mask):
    count = lax.axis_size(axis)
    return lax.ppermute(value, axis, [(i, i ^ mask) for i in range(count)])


def call(body, outs, *args, specs=None, after=(), flag=False, cost=0, scratch=()):
    specs = specs or [VMEM] * len(args)
    outs = list(outs) + [((8, 128), F32)] * flag

    def kernel(*refs):
        refs = list(refs[: len(args)] + refs[len(args) + len(after) :])
        if flag:
            ref = refs.pop(len(args) + len(outs) - 1)
            ref[...] = jnp.zeros(ref.shape, F32)
        body(*refs)

    moved = sum(a.size * a.dtype.itemsize for a in args)
    return pl.pallas_call(
        kernel,
        out_shape=[jax.ShapeDtypeStruct(shape, dtype) for shape, dtype in outs],
        in_specs=specs + [VMEM] * len(after),
        out_specs=[VMEM] * len(outs),
        scratch_shapes=list(scratch),
        compiler_params=pltpu.CompilerParams(vmem_limit_bytes=VMEM_LIMIT),
        cost_estimate=pl.CostEstimate(flops=cost, bytes_accessed=moved, transcendentals=0),
    )(*args, *after)


SENT = ((1, 0), (2, 0), (3, 1), (2, 1))
KEPT = ((0, 0), (3, 0), (0, 1), (1, 1))


def products(here_ref, a_ref, b_ref, out_refs, held, sems, parts):
    rows = held.shape[0] // (len(parts) * len(SENT))
    copies = []
    for own, order in parts:
        base = (here_ref[2] if own else 1 - here_ref[2]) * 8
        for owner, part in order:
            start = (base + lax.bitwise_xor(here_ref[0], owner) * 2 + part) * rows
            to = held.at[pl.ds(rows * len(copies), rows), :]
            copies.append(
                pltpu.make_async_copy(a_ref.at[pl.ds(pl.multiple_of(start, rows), rows), :], to, sems.at[len(copies)])
            )
    for copy in copies:
        copy.start()
    per = len(SENT)
    for o, out_ref in enumerate(out_refs):
        for copy in copies[o * per : (o + 1) * per]:
            copy.wait()
        here = held[o * per * rows : (o + 1) * per * rows, :]
        out_ref[: per * rows, :] = jnp.dot(here, b_ref[...], preferred_element_type=F32)


def product_scratch(pair_elements, parts):
    rows, depth = pair_elements.shape
    return [pltpu.VMEM((rows // 4 * parts, depth), BF16), pltpu.SemaphoreType.DMA((4 * parts,))]


def pack(ref, value):
    rows = value.shape[0]
    top = jnp.maximum(jnp.max(jnp.abs(value), axis=0, keepdims=True), 1e-30)
    level = jnp.clip(jnp.ceil(jnp.log2(top * (1.0 / 32000.0)) * 256.0), -32000.0, 32000.0)
    scaled = value * jnp.exp2(level * (-1.0 / 256.0))
    ref[:rows, :] = jnp.round(scaled).astype(jnp.int32).astype(I16)
    ref[rows:, :] = jnp.broadcast_to(level, (TAIL, value.shape[1])).astype(jnp.int32).astype(I16)


def unpack(ref):
    rows = ref.shape[0] - TAIL
    level = ref[rows:, :].astype(jnp.int32).astype(F32)[0:1, :]
    return ref[:rows, :].astype(jnp.int32).astype(F32) * jnp.exp2(level * (1.0 / 256.0))


def first_messages(own_ref, other_ref, a_ref, b_ref):
    rows = own_ref.shape[0] // 2
    pack(a_ref, own_ref[:rows, :] + other_ref[:rows, :])
    pack(b_ref, own_ref[rows:, :] + other_ref[rows : 2 * rows, :])


def second_messages(own_ref, other_ref, a_in, b_in, kept_ref, a_ref, b_ref):
    rows = own_ref.shape[0] // 4
    for part, (came, out) in enumerate(((a_in, a_ref), (b_in, b_ref))):
        at = 2 * part * rows
        total = own_ref[at : at + 2 * rows, :] + other_ref[at : at + 2 * rows, :] + unpack(came)
        kept_ref[part * rows : (part + 1) * rows, :] = total[:rows, :]
        pack(out, total[rows:, :])


def split_four(mine, work_ref, own_ref, message_refs):
    quarter = work_ref.shape[0] // 4

    def rows_of(owner):
        return work_ref[pl.ds(pl.multiple_of(owner * quarter, quarter), quarter), :]

    own_ref[...] = rows_of(mine)
    for mask, out in enumerate(message_refs):
        pack(out, rows_of(lax.bitwise_xor(mine, mask + 1)))


def third_messages(here_ref, kept_ref, a_in, b_in, own_ref, m1_ref, m2_ref, m3_ref, work_ref):
    half = kept_ref.shape[0] // 2
    work_ref[:half, :] = kept_ref[:half, :] + unpack(a_in)
    work_ref[half:, :] = kept_ref[half:, :] + unpack(b_in)
    split_four(here_ref[1], work_ref, own_ref, (m1_ref, m2_ref, m3_ref))


def last_sum(own_ref, m1_in, m2_in, m3_in, out_ref):
    out_ref[...] = (own_ref[...] + unpack(m1_in) + unpack(m2_in) + unpack(m3_in)).astype(BF16)


def gram_messages(here_ref, mine_ref, came_ref, own_ref, m1_ref, m2_ref, m3_ref, work_ref):
    work_ref[...] = mine_ref[...] + came_ref[...]
    split_four(here_ref[3] // 2, work_ref, own_ref, (m1_ref, m2_ref, m3_ref))


def gram_halves(here_ref, own_ref, m1_in, m2_in, m3_in, kept_ref, out_ref, work_ref):
    rows = kept_ref.shape[0]
    work_ref[...] = own_ref[...] + unpack(m1_in) + unpack(m2_in) + unpack(m3_in)
    half = here_ref[3] % 2
    kept_ref[...] = work_ref[pl.ds(pl.multiple_of(half * rows, rows), rows), :]
    pack(out_ref, work_ref[pl.ds(pl.multiple_of((1 - half) * rows, rows), rows), :])


def fill_weights(val_table, freq_ref, other_freq, ci_ref, vi_ref, ce_ref, out_refs):
    shape = ci_ref.shape
    index = ci_ref[...]
    high, low = index // 128, index % 128
    cond = jnp.zeros(shape, F32)
    for row in range(ce_ref.shape[0]):
        table = jnp.broadcast_to(ce_ref[row : row + 1, :], shape)
        cond = jnp.where(high == row, jnp.take_along_axis(table, low, axis=1), cond)
    level = vi_ref[...]
    val = jnp.zeros(shape, F32)
    for row in range(val_table.shape[0]):
        val = jnp.where(level == row, val_table[row], val)
    spacing = cond - val
    for freq, out_ref in zip((freq_ref[0], other_freq), out_refs):
        out_ref[...] = 2.0 * spacing / (spacing * spacing + freq * freq)


def gram_step(here, weights, pieces, owners, grams, after=()):
    width = pieces[0].shape[1]
    count, kinds = len(pieces), len(weights)

    def body(here_ref, *refs):
        w_refs, came, before, out_refs = refs[:kinds], refs[kinds : kinds + count], refs[kinds + count : -kinds], refs[-kinds:]
        totals = [ref[...] for ref in before] or [None] * kinds
        for ref, (owner, masks) in zip(came, owners):
            first = (here_ref[2] * 4 + lax.bitwise_xor(here_ref[0], owner)) * 4
            parts = [[] for _ in range(kinds)]
            for j, mask in enumerate(masks):
                rows = ref[128 * j : 128 * (j + 1), :].astype(F32).T
                for part, w_ref in zip(parts, w_refs):
                    w = w_ref[pl.ds(first + lax.bitwise_xor(here_ref[1], mask), 1), :]
                    part.append((rows * w).astype(BF16))
            for kind, part in enumerate(parts):
                term = jnp.dot(jnp.concatenate(part, axis=1), ref[...], preferred_element_type=F32)
                totals[kind] = term if totals[kind] is None else totals[kind] + term
        for out_ref, total in zip(out_refs, totals):
            out_ref[...] = total

    return call(
        body,
        [((width, width), F32)] * kinds,
        here,
        *weights,
        *pieces,
        *grams,
        cost=2 * kinds * width * width * sum(p.shape[0] for p in pieces),
        specs=[SMEM] + [VMEM] * (kinds + count + len(grams)),
        after=after,
    )


def on_device(pair_elements, subspace, val_energy, cond_energy, val_index, cond_index, frequencies):
    here = jnp.stack([lax.axis_index(name).astype(jnp.int32) for name in PW + ("pair",)])
    rows, width = pair_elements.shape[0], subspace.shape[1]
    quarter, eighth, piece = rows // 4, rows // 8, rows // 32
    message = lambda count: ((count + TAIL, width), I16)
    sums = lambda count: ((count, width), F32)
    flops = 2 * quarter * pair_elements.shape[1] * width

    def first_products(here_ref, freq_ref, a_ref, b_ref, out_ref, held, sems):
        out_ref[quarter:, :] = jnp.full((8, width), freq_ref[0], F32)
        products(here_ref, a_ref, b_ref, (out_ref,), held, sems, [(False, SENT)])

    def second_products(here_ref, a_ref, b_ref, own_ref, other_ref, held, sems):
        products(here_ref, a_ref, b_ref, (own_ref, other_ref), held, sems, [(True, SENT), (False, KEPT)])

    sent_other, done = call(
        first_products,
        [sums(quarter + 8)],
        here,
        frequencies,
        pair_elements,
        subspace,
        specs=[SMEM, SMEM, ANY, VMEM],
        flag=True,
        cost=flops,
        scratch=product_scratch(pair_elements, 1),
    )
    sent_in = xor_permute(sent_other, "pw_c", 1)
    sent_own, kept_other = call(
        second_products,
        [sums(quarter)] * 2,
        here,
        pair_elements,
        subspace,
        specs=[SMEM, ANY, VMEM],
        after=[done],
        cost=2 * flops,
        scratch=product_scratch(pair_elements, 2),
    )
    kept_in = xor_permute(kept_other, "pw_c", 1)

    late = [sums(quarter), ((rows // 128, 128), F32), ((rows // 128, 128), F32)]

    def late_work(core, before, done):
        def body(here_ref, val_table, freq_ref, a_ref, b_ref, other_ref, ci_ref, vi_ref, ce_ref, *refs):
            old, (kept_ref, *w_refs), (held, sems) = refs[: len(before)], refs[len(before) : len(before) + 3], refs[-2:]

            @pl.when(here_ref[2] == core)
            def _():
                products(here_ref, a_ref, b_ref, (kept_ref,), held, sems, [(True, KEPT)])
                fill_weights(val_table, freq_ref, other_ref[0:1, 0:1], ci_ref, vi_ref, ce_ref, w_refs)

            if before:

                @pl.when(here_ref[2] != core)
                def _():
                    for old_ref, ref in zip(old, (kept_ref, *w_refs)):
                        ref[...] = old_ref[...]

        return call(
            body,
            late,
            here,
            val_energy,
            frequencies,
            pair_elements,
            subspace,
            other_frequency,
            cond_index.reshape(-1, 128),
            val_index.reshape(-1, 128),
            cond_energy.reshape(-1, 128),
            *before,
            specs=[SMEM] * 3 + [ANY] + [VMEM] * (5 + len(before)),
            after=done,
            flag=True,
            cost=flops,
            scratch=product_scratch(pair_elements, 1),
        )

    other_frequency = sent_in[quarter:, :128]
    *early, done = late_work(1, [], [])
    a, b, done = call(first_messages, [message(eighth)] * 2, sent_own, sent_in, after=[done], flag=True)
    kept_own, *weights, done = late_work(0, early, [done])

    a, b = xor_permute(a, "pw_x", 1), xor_permute(b, "pw_x", 3)
    kept, a, b = call(
        second_messages, [sums(eighth)] + [message(eighth // 2)] * 2, kept_own, kept_in, a, b
    )
    a, b = xor_permute(a, "pw_x", 3), xor_permute(b, "pw_x", 1)
    own, *out = call(
        third_messages,
        [sums(piece)] + [message(piece)] * 3,
        here,
        kept,
        a,
        b,
        specs=[SMEM] + [VMEM] * 3,
        scratch=[pltpu.VMEM((eighth, width), F32)],
    )
    came = [xor_permute(value, "pw_z", mask + 1) for mask, value in enumerate(out)]
    coeffs = call(last_sum, [((piece, width), BF16)], own, *came)[0]

    whole = jnp.concatenate([coeffs] + [xor_permute(coeffs, "pw_z", mask) for mask in (1, 2, 3)], axis=0)
    near, far = xor_permute(whole, "pw_x", 1), xor_permute(whole, "pw_x", 3)
    grams = gram_step(here, weights, [whole], [(0, (0, 1, 2, 3))], [])
    near, far, grams = lax.optimization_barrier((near, far, grams))
    top = xor_permute(far[: eighth // 2], "pw_x", 1)
    bottom = xor_permute(near[eighth // 2 :], "pw_x", 3)
    grams = gram_step(here, weights, [near, far], [(1, (0, 1, 2, 3)), (3, (0, 1, 2, 3))], grams)
    mine, theirs = gram_step(here, weights, [top, bottom], [(2, (0, 1)), (2, (2, 3))], grams)

    part = width // 4
    own, *out = call(
        gram_messages,
        [sums(part)] + [message(part)] * 3,
        here,
        mine,
        xor_permute(theirs, "pw_c", 1),
        specs=[SMEM] + [VMEM] * 2,
        scratch=[pltpu.VMEM((width, width), F32)],
    )
    came = [xor_permute(value, "pair", 2 * (mask + 1)) for mask, value in enumerate(out)]
    own, out = call(
        gram_halves,
        [sums(part // 2), message(part // 2)],
        here,
        own,
        *came,
        specs=[SMEM] + [VMEM] * 4,
        scratch=[pltpu.VMEM((part, width), F32)],
    )
    factor = -4.0 / (rows * lax.axis_size("pair"))

    def finish(own_ref, came_ref, out_ref):
        out_ref[...] = (own_ref[...] + unpack(came_ref)) * factor

    return call(finish, [sums(part // 2)], own, xor_permute(out, "pair", 1))[0][None]


def solution(mesh):
    torus = Mesh(mesh.devices.reshape(mesh.shape["pair"], 4, 4, 2), ("pair",) + PW)
    return jax.shard_map(
        on_device,
        mesh=torus,
        in_specs=(P("pair", PW), P(PW, None), P(), P(), P("pair"), P("pair"), P(PW)),
        out_specs=P(PW, "pair", None),
        check_vma=False,
    )
```

```python
import jax
import jax.numpy as jnp
from jax import lax
from jax.experimental import pallas as pl
from jax.experimental.pallas import tpu as pltpu
from jax.sharding import Mesh
from jax.sharding import PartitionSpec as P

PW = ("pw_x", "pw_z", "pw_c")
F32, BF16, I16 = jnp.float32, jnp.bfloat16, jnp.int16
TAIL = 16
Z_ORDER, Y_ORDER = (3, 2, 1), (2, 3, 1)
VMEM_LIMIT, VMEM_LARGE = 24 * 1024 * 1024, 46 * 1024 * 1024
SMEM, VMEM = pl.BlockSpec(memory_space=pltpu.SMEM), pl.BlockSpec(memory_space=pltpu.VMEM)
ANY = pl.BlockSpec(memory_space=pl.ANY)


def xor_permute(value, axis, mask):
    count = lax.axis_size(axis)
    return lax.ppermute(value, axis, [(i, i ^ mask) for i in range(count)])


def call(body, outs, *args, specs=None, after=(), flag=False, scratch=(), limit=VMEM_LIMIT):
    specs = specs or [VMEM] * len(args)
    outs = list(outs) + [((8, 128), F32)] * flag

    def kernel(*refs):
        refs = list(refs[: len(args)] + refs[len(args) + len(after) :])
        if flag:
            ref = refs.pop(len(args) + len(outs) - 1)
            ref[...] = jnp.zeros(ref.shape, F32)
        body(*refs)

    return pl.pallas_call(
        kernel,
        out_shape=[jax.ShapeDtypeStruct(shape, dtype) for shape, dtype in outs],
        in_specs=specs + [VMEM] * len(after),
        out_specs=[VMEM] * len(outs),
        scratch_shapes=list(scratch),
        compiler_params=pltpu.CompilerParams(vmem_limit_bytes=limit),
        cost_estimate=pl.CostEstimate(flops=0, bytes_accessed=0, transcendentals=0),
    )(*args, *after)


def products(here_ref, a_ref, b_ref, held, sems, parts):
    rows = held.shape[0] // len(parts)
    copies = []
    for i, (own, owner, _, _) in enumerate(parts):
        core = here_ref[2] if own else 1 - here_ref[2]
        start = (core * 4 + lax.bitwise_xor(here_ref[0], owner)) * rows
        block = a_ref.at[pl.ds(pl.multiple_of(start, rows), rows), :]
        copies.append(pltpu.make_async_copy(block, held.at[pl.ds(rows * i, rows), :], sems.at[i]))
    for copy in copies:
        copy.start()
    for i, (_, _, out_ref, to) in enumerate(parts):
        copies[i].wait()
        here = held[rows * i : rows * (i + 1), :]
        out_ref[to : to + rows, :] = jnp.dot(here, b_ref[...], preferred_element_type=F32)


def product_scratch(pair_elements, parts):
    rows, depth = pair_elements.shape
    return [pltpu.VMEM((rows // 8 * parts, depth), BF16), pltpu.SemaphoreType.DMA((parts,))]


def pack(ref, value):
    rows = value.shape[0]
    top = jnp.maximum(jnp.max(jnp.abs(value), axis=0, keepdims=True), 1e-30)
    level = jnp.clip(jnp.ceil(jnp.log2(top * (1.0 / 32000.0)) * 256.0), -32000.0, 32000.0)
    scaled = value * jnp.exp2(level * (-1.0 / 256.0))
    ref[:rows, :] = jnp.round(scaled).astype(jnp.int32).astype(I16)
    ref[rows:, :] = jnp.broadcast_to(level, (TAIL, value.shape[1])).astype(jnp.int32).astype(I16)


def unpack(ref):
    rows = ref.shape[0] - TAIL
    level = ref[rows:, :].astype(jnp.int32).astype(F32)[0:1, :]
    return ref[:rows, :].astype(jnp.int32).astype(F32) * jnp.exp2(level * (1.0 / 256.0))


def x_messages(own_ref, other_ref, *out_refs):
    rows = own_ref.shape[0] // len(out_refs)
    for i, out in enumerate(out_refs):
        pack(out, own_ref[rows * i : rows * (i + 1), :] + other_ref[rows * i : rows * (i + 1), :])


def split_four(mine, work_ref, own_ref, message_refs, masks):
    quarter = work_ref.shape[0] // 4

    def rows_of(owner):
        return work_ref[pl.ds(pl.multiple_of(owner * quarter, quarter), quarter), :]

    for mask, out in zip(masks, message_refs):
        pack(out, rows_of(lax.bitwise_xor(mine, mask)))
    own_ref[...] = rows_of(mine)


def z_messages(here_ref, own_ref, other_ref, m1_in, m2_in, m3_in, out_ref, m1_ref, m2_ref, m3_ref, work_ref):
    work_ref[...] = own_ref[...] + other_ref[...] + unpack(m1_in) + unpack(m2_in) + unpack(m3_in)
    split_four(here_ref[1], work_ref, out_ref, (m1_ref, m2_ref, m3_ref), Z_ORDER)


def last_sum(own_ref, m1_in, m2_in, m3_in, out_ref):
    out_ref[...] = (own_ref[...] + unpack(m1_in) + unpack(m2_in) + unpack(m3_in)).astype(BF16)


def gram_messages(here_ref, mine_ref, came_ref, own_ref, m1_ref, m2_ref, m3_ref, work_ref):
    work_ref[...] = mine_ref[...] + came_ref[...]
    split_four(here_ref[3] // 2, work_ref, own_ref, (m1_ref, m2_ref, m3_ref), Y_ORDER)


def gram_halves(here_ref, own_ref, m1_in, m2_in, m3_in, kept_ref, out_ref, work_ref):
    rows = kept_ref.shape[0]
    work_ref[...] = own_ref[...] + unpack(m1_in) + unpack(m2_in) + unpack(m3_in)
    half = here_ref[3] % 2
    kept_ref[...] = work_ref[pl.ds(pl.multiple_of(half * rows, rows), rows), :]
    pack(out_ref, work_ref[pl.ds(pl.multiple_of((1 - half) * rows, rows), rows), :])


def fill_weights(val_table, freq_ref, other_freq, ci_ref, vi_ref, ce_ref, out_refs):
    shape = ci_ref.shape
    index = ci_ref[...]
    high, low = index // 128, index % 128
    cond = jnp.zeros(shape, F32)
    for row in range(ce_ref.shape[0]):
        table = jnp.broadcast_to(ce_ref[row : row + 1, :], shape)
        cond = jnp.where(high == row, jnp.take_along_axis(table, low, axis=1), cond)
    level = vi_ref[...]
    val = jnp.zeros(shape, F32)
    for row in range(val_table.shape[0]):
        val = jnp.where(level == row, val_table[row], val)
    spacing = cond - val
    for freq, out_ref in zip((freq_ref[0], other_freq), out_refs):
        out_ref[...] = 2.0 * spacing / (spacing * spacing + freq * freq)


def gram_step(here, weights, pieces, owners, grams, after=()):
    width = pieces[0].shape[1]
    count, kinds = len(pieces), len(weights)

    def body(here_ref, *refs):
        w_refs, came, before, out_refs = refs[:kinds], refs[kinds : kinds + count], refs[kinds + count : -kinds], refs[-kinds:]
        totals = [ref[...] for ref in before] or [None] * kinds
        for ref, (owner, masks) in zip(came, owners):
            first = (here_ref[2] * 4 + lax.bitwise_xor(here_ref[0], owner)) * 4
            parts = [[] for _ in range(kinds)]
            for j, mask in enumerate(masks):
                rows = ref[128 * j : 128 * (j + 1), :].astype(F32).T
                for part, w_ref in zip(parts, w_refs):
                    w = w_ref[pl.ds(first + lax.bitwise_xor(here_ref[1], mask), 1), :]
                    part.append((rows * w).astype(BF16))
            for kind, part in enumerate(parts):
                term = jnp.dot(jnp.concatenate(part, axis=1), ref[...], preferred_element_type=F32)
                totals[kind] = term if totals[kind] is None else totals[kind] + term
        for out_ref, total in zip(out_refs, totals):
            out_ref[...] = total

    return call(
        body,
        [((width, width), F32)] * kinds,
        here,
        *weights,
        *pieces,
        *grams,
        specs=[SMEM] + [VMEM] * (kinds + count + len(grams)),
        after=after,
    )


def on_device(pair_elements, subspace, val_energy, cond_energy, val_index, cond_index, frequencies):
    here = jnp.stack([lax.axis_index(name).astype(jnp.int32) for name in PW + ("pair",)])
    rows, width = pair_elements.shape[0], subspace.shape[1]
    eighth, piece = rows // 8, rows // 32
    message = lambda count: ((count + TAIL, width), I16)
    sums = lambda count: ((count, width), F32)

    def product_call(body, outs, *args, after=(), flag=False, parts=1):
        specs = [SMEM] * (len(args) + 1) + [ANY, VMEM]
        scratch = product_scratch(pair_elements, parts)
        arrays = (here, *args, pair_elements, subspace)
        return call(body, outs, *arrays, specs=specs, after=after, flag=flag, scratch=scratch, limit=VMEM_LARGE)

    def far_other(here_ref, freq_ref, a_ref, b_ref, out_ref, held, sems):
        out_ref[eighth:, :] = jnp.full((8, width), freq_ref[0], F32)
        products(here_ref, a_ref, b_ref, held, sems, [(False, 2, out_ref, 0)])

    def far_own(here_ref, a_ref, b_ref, far_ref, near_ref, kept_ref, held, sems):
        parts = [(True, 2, far_ref, 0), (False, 1, near_ref, 0), (False, 3, near_ref, eighth), (False, 0, kept_ref, 0)]
        products(here_ref, a_ref, b_ref, held, sems, parts)

    def near_messages(here_ref, a_ref, b_ref, other_ref, one_ref, three_ref, held, sems, own_ref):
        products(here_ref, a_ref, b_ref, held, sems, [(True, 1, own_ref, 0), (True, 3, own_ref, eighth)])
        x_messages(own_ref, other_ref, one_ref, three_ref)

    def rest(here_ref, val_table, freq_ref, a_ref, b_ref, other_ref, ci_ref, vi_ref, ce_ref, *refs):
        (kept_ref, *w_refs), (held, sems) = refs[:3], refs[3:]
        products(here_ref, a_ref, b_ref, held, sems, [(True, 0, kept_ref, 0)])
        fill_weights(val_table, freq_ref, other_ref[0:1, 0:1], ci_ref, vi_ref, ce_ref, w_refs)

    other, done = product_call(far_other, [sums(eighth + 8)], frequencies, flag=True)
    far_in = xor_permute(other, "pw_c", 1)
    own, near_other, kept_other = product_call(
        far_own, [sums(eighth), sums(2 * eighth), sums(eighth)], after=[done], parts=4
    )
    near_other, far_in = lax.optimization_barrier((near_other, far_in))
    near_in, kept_in = xor_permute(near_other, "pw_c", 1), xor_permute(kept_other, "pw_c", 1)
    far, done = call(x_messages, [message(eighth)], own, far_in, flag=True)
    far = xor_permute(far, "pw_x", 2)
    near1, near3, done = call(
        near_messages,
        [message(eighth)] * 2,
        here,
        pair_elements,
        subspace,
        near_in,
        specs=[SMEM, ANY, VMEM, VMEM],
        after=[done],
        flag=True,
        scratch=product_scratch(pair_elements, 2) + [pltpu.VMEM((2 * eighth, width), F32)],
        limit=VMEM_LARGE,
    )
    near1, near3 = xor_permute(near1, "pw_x", 1), xor_permute(near3, "pw_x", 3)
    kept, *weights = call(
        rest,
        [sums(eighth), ((rows // 128, 128), F32), ((rows // 128, 128), F32)],
        here,
        val_energy,
        frequencies,
        pair_elements,
        subspace,
        far_in[eighth:, :128],
        cond_index.reshape(-1, 128),
        val_index.reshape(-1, 128),
        cond_energy.reshape(-1, 128),
        specs=[SMEM] * 3 + [ANY] + [VMEM] * 5,
        after=[done],
        scratch=product_scratch(pair_elements, 1),
        limit=VMEM_LARGE,
    )

    own, *out = call(
        z_messages,
        [sums(piece)] + [message(piece)] * 3,
        here,
        kept,
        kept_in,
        far,
        near1,
        near3,
        specs=[SMEM] + [VMEM] * 5,
        scratch=[pltpu.VMEM((eighth, width), F32)],
    )
    came = [xor_permute(value, "pw_z", mask) for mask, value in zip(Z_ORDER, out)]
    coeffs = call(last_sum, [((piece, width), BF16)], own, *came)[0]

    whole = jnp.concatenate([coeffs] + [xor_permute(coeffs, "pw_z", mask) for mask in (1, 2, 3)], axis=0)
    near, far = xor_permute(whole, "pw_x", 1), xor_permute(whole, "pw_x", 3)
    grams = gram_step(here, weights, [whole], [(0, (0, 1, 2, 3))], [])
    near, far, grams = lax.optimization_barrier((near, far, grams))
    top = xor_permute(far[: eighth // 2], "pw_x", 1)
    bottom = xor_permute(near[eighth // 2 :], "pw_x", 3)
    grams = gram_step(here, weights, [near, far], [(1, (0, 1, 2, 3)), (3, (0, 1, 2, 3))], grams)
    mine, theirs = gram_step(here, weights, [top, bottom], [(2, (0, 1)), (2, (2, 3))], grams)

    part = width // 4
    own, *out = call(
        gram_messages,
        [sums(part)] + [message(part)] * 3,
        here,
        mine,
        xor_permute(theirs, "pw_c", 1),
        specs=[SMEM] + [VMEM] * 2,
        scratch=[pltpu.VMEM((width, width), F32)],
    )
    came = [xor_permute(value, "pair", 2 * mask) for mask, value in zip(Y_ORDER, out)]
    own, out = call(
        gram_halves,
        [sums(part // 2), message(part // 2)],
        here,
        own,
        *came,
        specs=[SMEM] + [VMEM] * 4,
        scratch=[pltpu.VMEM((part, width), F32)],
    )
    factor = -4.0 / (rows * lax.axis_size("pair"))

    def finish(own_ref, came_ref, out_ref):
        out_ref[...] = (own_ref[...] + unpack(came_ref)) * factor

    return call(finish, [sums(part // 2)], own, xor_permute(out, "pair", 1))[0][None]


def solution(mesh):
    torus = Mesh(mesh.devices.reshape(mesh.shape["pair"], 4, 4, 2), ("pair",) + PW)
    return jax.shard_map(
        on_device,
        mesh=torus,
        in_specs=(P("pair", PW), P(PW, None), P(), P(), P("pair"), P("pair"), P(PW)),
        out_specs=P(PW, "pair", None),
        check_vma=False,
    )
```

```python
import jax
import jax.numpy as jnp
from jax import lax
from jax.experimental import pallas as pl
from jax.experimental.pallas import tpu as pltpu
from jax.sharding import Mesh
from jax.sharding import PartitionSpec as P

PW = ("pw_x", "pw_z", "pw_c")
F32, BF16, I16 = jnp.float32, jnp.bfloat16, jnp.int16
TAIL = 16
Z_ORDER, Y_ORDER = (3, 2, 1), (2, 3, 1)
VMEM_LIMIT, VMEM_LARGE = 24 * 1024 * 1024, 46 * 1024 * 1024
SMEM, VMEM = pl.BlockSpec(memory_space=pltpu.SMEM), pl.BlockSpec(memory_space=pltpu.VMEM)
ANY = pl.BlockSpec(memory_space=pl.ANY)


def xor_permute(value, axis, mask):
    count = lax.axis_size(axis)
    return lax.ppermute(value, axis, [(i, i ^ mask) for i in range(count)])


def call(body, outs, *args, specs=None, after=(), flag=False, cost=0, scratch=(), limit=VMEM_LIMIT):
    specs = specs or [VMEM] * len(args)
    moved = sum(a.size * a.dtype.itemsize for a in args)
    outs = list(outs) + [((8, 128), F32)] * flag

    def kernel(*refs):
        refs = list(refs[: len(args)] + refs[len(args) + len(after) :])
        if flag:
            ref = refs.pop(len(args) + len(outs) - 1)
            ref[...] = jnp.zeros(ref.shape, F32)
        body(*refs)

    return pl.pallas_call(
        kernel,
        out_shape=[jax.ShapeDtypeStruct(shape, dtype) for shape, dtype in outs],
        in_specs=specs + [VMEM] * len(after),
        out_specs=[VMEM] * len(outs),
        scratch_shapes=list(scratch),
        compiler_params=pltpu.CompilerParams(vmem_limit_bytes=limit),
        cost_estimate=pl.CostEstimate(flops=cost, bytes_accessed=moved, transcendentals=0),
    )(*args, *after)


SENT = ((1, 0), (2, 0), (3, 1), (2, 1))
KEPT = ((0, 0), (3, 0), (0, 1), (1, 1))


def products(here_ref, a_ref, b_ref, out_refs, held, sems, parts):
    order = SENT + KEPT
    per = len(order)
    rows = held.shape[0] // (len(parts) * per)
    copies = []
    for own, stream in parts:
        base = (here_ref[2] if own else 1 - here_ref[2]) * 16 + stream * 2
        for owner, part in order:
            start = (base + lax.bitwise_xor(here_ref[0], owner) * 4 + part) * rows
            to = held.at[pl.ds(rows * len(copies), rows), :]
            copies.append(
                pltpu.make_async_copy(a_ref.at[pl.ds(pl.multiple_of(start, rows), rows), :], to, sems.at[len(copies)])
            )
    for copy in copies:
        copy.start()
    for o, out_ref in enumerate(out_refs):
        for copy in copies[o * per : (o + 1) * per]:
            copy.wait()
        here = held[o * per * rows : (o + 1) * per * rows, :]
        out_ref[: per * rows, :] = jnp.dot(here, b_ref[...], preferred_element_type=F32)


def product_scratch(pair_elements, parts):
    rows, depth = pair_elements.shape
    return [pltpu.VMEM((rows // 4 * parts, depth), BF16), pltpu.SemaphoreType.DMA((8 * parts,))]


def pack(ref, value):
    rows = value.shape[0]
    top = jnp.maximum(jnp.max(jnp.abs(value), axis=0, keepdims=True), 1e-30)
    level = jnp.clip(jnp.ceil(jnp.log2(top * (1.0 / 32000.0)) * 256.0), -32000.0, 32000.0)
    scaled = value * jnp.exp2(level * (-1.0 / 256.0))
    ref[:rows, :] = jnp.round(scaled).astype(jnp.int32).astype(I16)
    ref[rows:, :] = jnp.broadcast_to(level, (TAIL, value.shape[1])).astype(jnp.int32).astype(I16)


def unpack(ref):
    rows = ref.shape[0] - TAIL
    level = ref[rows:, :].astype(jnp.int32).astype(F32)[0:1, :]
    return ref[:rows, :].astype(jnp.int32).astype(F32) * jnp.exp2(level * (1.0 / 256.0))


def first_messages(own_ref, other_ref, kept_ref, a_ref, b_ref):
    rows = own_ref.shape[0] // 4
    pack(a_ref, own_ref[:rows, :] + other_ref[:rows, :])
    pack(b_ref, own_ref[rows : 2 * rows, :] + other_ref[rows : 2 * rows, :])
    kept_ref[...] = own_ref[2 * rows :, :] + other_ref[2 * rows : 4 * rows, :]


def second_messages(sum_ref, a_in, b_in, kept_ref, a_ref, b_ref):
    rows = sum_ref.shape[0] // 4
    for part, (came, out) in enumerate(((a_in, a_ref), (b_in, b_ref))):
        at = 2 * part * rows
        total = sum_ref[at : at + 2 * rows, :] + unpack(came)
        kept_ref[part * rows : (part + 1) * rows, :] = total[:rows, :]
        pack(out, total[rows:, :])


def split_four(mine, work_ref, own_ref, message_refs, masks):
    quarter = work_ref.shape[0] // 4

    def rows_of(owner):
        return work_ref[pl.ds(pl.multiple_of(owner * quarter, quarter), quarter), :]

    for mask, out in zip(masks, message_refs):
        pack(out, rows_of(lax.bitwise_xor(mine, mask)))
    own_ref[...] = rows_of(mine)


def third_messages(here_ref, kept_ref, a_in, b_in, own_ref, m1_ref, m2_ref, m3_ref, work_ref):
    half = kept_ref.shape[0] // 2
    work_ref[:half, :] = kept_ref[:half, :] + unpack(a_in)
    work_ref[half:, :] = kept_ref[half:, :] + unpack(b_in)
    split_four(here_ref[1], work_ref, own_ref, (m1_ref, m2_ref, m3_ref), Z_ORDER)


def last_sum(own_ref, m1_in, m2_in, m3_in, out_ref):
    out_ref[...] = (own_ref[...] + unpack(m1_in) + unpack(m2_in) + unpack(m3_in)).astype(BF16)


def join(p0_ref, p1_ref, p2_ref, p3_ref, out_ref):
    rows = p0_ref.shape[0]
    for i, ref in enumerate((p0_ref, p1_ref, p2_ref, p3_ref)):
        out_ref[rows * i : rows * (i + 1), :] = ref[...]


def gram_messages(here_ref, mine_ref, came_ref, own_ref, m1_ref, m2_ref, m3_ref, work_ref):
    work_ref[...] = mine_ref[...] + came_ref[...]
    split_four(here_ref[3] // 2, work_ref, own_ref, (m1_ref, m2_ref, m3_ref), Y_ORDER)


def gram_halves(here_ref, own_ref, m1_in, m2_in, m3_in, kept_ref, out_ref, work_ref):
    rows = kept_ref.shape[0]
    work_ref[...] = own_ref[...] + unpack(m1_in) + unpack(m2_in) + unpack(m3_in)
    half = here_ref[3] % 2
    kept_ref[...] = work_ref[pl.ds(pl.multiple_of(half * rows, rows), rows), :]
    pack(out_ref, work_ref[pl.ds(pl.multiple_of((1 - half) * rows, rows), rows), :])


def weights_kernel(here_ref, val_table, freq_ref, other_ref, ci_ref, vi_ref, ce_ref, *out_refs):
    shape = ci_ref.shape
    half = shape[1] // 2
    index = ci_ref[...]
    high, low = index // 128, index % 128
    cond = jnp.zeros(shape, F32)
    for row in range(ce_ref.shape[0]):
        table = jnp.broadcast_to(ce_ref[row : row + 1, :], shape)
        cond = jnp.where(high == row, jnp.take_along_axis(table, low, axis=1), cond)
    level = vi_ref[...]
    val = jnp.zeros(shape, F32)
    for row in range(val_table.shape[0]):
        val = jnp.where(level == row, val_table[row], val)
    spacing = cond - val
    swapped = jnp.concatenate([spacing[:, half:], spacing[:, :half]], axis=1)
    spacing = jnp.where(here_ref[1] % 2 == 1, swapped, spacing)
    for freq, out_ref in zip((freq_ref[0], other_ref[0:1, 0:1]), out_refs):
        out_ref[...] = 2.0 * spacing / (spacing * spacing + freq * freq)


def gram_step(here, weights, pieces, places, grams, after=()):
    width = pieces[0].shape[1]
    count, kinds = len(pieces), len(weights)

    def body(here_ref, *refs):
        w_refs, came, before, out_refs = refs[:kinds], refs[kinds : kinds + count], refs[kinds + count : -kinds], refs[-kinds:]
        totals = [ref[...] for ref in before] or [None] * kinds
        for ref, (stream, owner) in zip(came, places):
            first = (here_ref[2] * 4 + lax.bitwise_xor(here_ref[0], owner)) * 4 + stream * 2
            parts = [[] for _ in range(kinds)]
            for j in range(2):
                rows = ref[128 * j : 128 * (j + 1), :].astype(F32).T
                for part, w_ref in zip(parts, w_refs):
                    w = w_ref[pl.ds(first + lax.bitwise_xor(here_ref[1] // 2, j), 1), :]
                    part.append((rows * w).astype(BF16))
            for kind, part in enumerate(parts):
                term = jnp.dot(jnp.concatenate(part, axis=1), ref[...], preferred_element_type=F32)
                totals[kind] = term if totals[kind] is None else totals[kind] + term
        for out_ref, total in zip(out_refs, totals):
            out_ref[...] = total

    return call(
        body,
        [((width, width), F32)] * kinds,
        here,
        *weights,
        *pieces,
        *grams,
        cost=2 * kinds * width * width * sum(p.shape[0] for p in pieces),
        specs=[SMEM] + [VMEM] * (kinds + count + len(grams)),
        after=after,
    )


def on_device(pair_elements, subspace, val_energy, cond_energy, val_index, cond_index, frequencies):
    here = jnp.stack([lax.axis_index(name).astype(jnp.int32) for name in PW + ("pair",)])
    rows, width = pair_elements.shape[0], subspace.shape[1]
    unit = rows // 64
    message = lambda count: ((count + TAIL, width), I16)
    sums = lambda count: ((count, width), F32)
    both = range(2)

    def product_call(body, outs, *args, after=(), flag=False, parts=1):
        specs = [SMEM] * (len(args) + 1) + [ANY, VMEM]
        scratch, cost = product_scratch(pair_elements, parts), 2 * parts * 16 * unit * pair_elements.shape[1] * width
        arrays = (here, *args, pair_elements, subspace)
        return call(body, outs, *arrays, specs=specs, after=after, flag=flag, cost=cost, scratch=scratch, limit=VMEM_LARGE)

    def first_other(here_ref, freq_ref, a_ref, b_ref, out_ref, held, sems):
        out_ref[16 * unit :, :] = jnp.full((8, width), freq_ref[0], F32)
        products(here_ref, a_ref, b_ref, (out_ref,), held, sems, [(False, 0)])

    def first_own(here_ref, a_ref, b_ref, own_ref, other_ref, held, sems):
        products(here_ref, a_ref, b_ref, (own_ref, other_ref), held, sems, [(True, 0), (False, 1)])

    def second_own(here_ref, a_ref, b_ref, own_ref, held, sems):
        products(here_ref, a_ref, b_ref, (own_ref,), held, sems, [(True, 1)])

    kept, a, b = [None] * 2, [None] * 2, [None] * 2
    first = [sums(8 * unit)] + [message(4 * unit)] * 2
    other, done = product_call(first_other, [sums(16 * unit + 8)], frequencies, flag=True)
    other_in = xor_permute(other, "pw_c", 1)
    own, other = product_call(first_own, [sums(16 * unit)] * 2, after=[done], parts=2)
    other, other_in = lax.optimization_barrier((other, other_in))
    kept[0], a[0], b[0], done = call(first_messages, first, own, other_in, flag=True)
    own = product_call(second_own, [sums(16 * unit)], after=[done])[0]
    kept[1], a[1], b[1] = call(first_messages, first, own, xor_permute(other, "pw_c", 1))

    last = None
    for s in both:
        a[s], b[s] = xor_permute(a[s], "pw_x", 1), xor_permute(b[s], "pw_x", 3)
    for s in both:
        after = [] if last is None else [last]
        kept[s], a[s], b[s], last = call(
            second_messages, [sums(4 * unit)] + [message(2 * unit)] * 2, kept[s], a[s], b[s], after=after, flag=True
        )
        a[s], b[s] = xor_permute(a[s], "pw_x", 3), xor_permute(b[s], "pw_x", 1)
    came = [None] * 2
    for s in both:
        own, *out, last = call(
            third_messages,
            [sums(unit)] + [message(unit)] * 3,
            here,
            kept[s],
            a[s],
            b[s],
            specs=[SMEM] + [VMEM] * 3,
            after=[last],
            flag=True,
            scratch=[pltpu.VMEM((4 * unit, width), F32)],
        )
        came[s] = [own] + [xor_permute(value, "pw_z", mask) for mask, value in zip(Z_ORDER, out)]
    weights = call(
        weights_kernel,
        [((rows // 128, 128), F32)] * 2,
        here,
        val_energy,
        frequencies,
        other_in[16 * unit :, :128],
        cond_index.reshape(-1, 128),
        val_index.reshape(-1, 128),
        cond_energy.reshape(-1, 128),
        specs=[SMEM] * 3 + [VMEM] * 4,
        after=[last],
    )

    last = weights[0]
    pieces = [None] * 2
    for s in both:
        own, last = call(last_sum, [((unit, width), BF16)], *came[s], after=[last], flag=True)
        pieces[s] = [own] + [xor_permute(own, "pw_z", mask) for mask in (1, 2, 3)]
    quarters, near, far = [None] * 2, [None] * 2, [None] * 2
    for s in both:
        quarters[s], last = call(join, [((4 * unit, width), BF16)], *pieces[s], after=[last], flag=True)
        near[s], far[s] = xor_permute(quarters[s], "pw_x", 1), xor_permute(quarters[s], "pw_x", 3)
        near[s], far[s] = lax.optimization_barrier((near[s], far[s]))
    across = [xor_permute(far[0], "pw_x", 1), xor_permute(near[1], "pw_x", 3)]
    grams = gram_step(here, weights, quarters, [(0, 0), (1, 0)], [])
    grams = gram_step(here, weights, [near[0], far[0]], [(0, 1), (0, 3)], grams)
    grams = gram_step(here, weights, [near[1], far[1], across[0]], [(1, 1), (1, 3), (0, 2)], grams)
    mine, theirs = gram_step(here, weights, [across[1]], [(1, 2)], grams)

    part = width // 4
    own, *out = call(
        gram_messages,
        [sums(part)] + [message(part)] * 3,
        here,
        mine,
        xor_permute(theirs, "pw_c", 1),
        specs=[SMEM] + [VMEM] * 2,
        scratch=[pltpu.VMEM((width, width), F32)],
    )
    came = [xor_permute(value, "pair", 2 * mask) for mask, value in zip(Y_ORDER, out)]
    own, out = call(
        gram_halves,
        [sums(part // 2), message(part // 2)],
        here,
        own,
        *came,
        specs=[SMEM] + [VMEM] * 4,
        scratch=[pltpu.VMEM((part, width), F32)],
    )
    factor = -4.0 / (rows * lax.axis_size("pair"))

    def finish(own_ref, came_ref, out_ref):
        out_ref[...] = (own_ref[...] + unpack(came_ref)) * factor

    return call(finish, [sums(part // 2)], own, xor_permute(out, "pair", 1))[0][None]


def solution(mesh):
    torus = Mesh(mesh.devices.reshape(mesh.shape["pair"], 4, 4, 2), ("pair",) + PW)
    return jax.shard_map(
        on_device,
        mesh=torus,
        in_specs=(P("pair", PW), P(PW, None), P(), P(), P("pair"), P("pair"), P(PW)),
        out_specs=P(PW, "pair", None),
        check_vma=False,
    )
```

```python
import jax
import jax.numpy as jnp
from jax import lax
from jax.experimental import pallas as pl
from jax.experimental.pallas import tpu as pltpu
from jax.sharding import Mesh
from jax.sharding import PartitionSpec as P

PW = ("pw_x", "pw_z", "pw_c")
F32, BF16, I16 = jnp.float32, jnp.bfloat16, jnp.int16
TAIL = 16
Z_ORDER, Y_ORDER = (3, 2, 1), (2, 3, 1)
VMEM_LIMIT, VMEM_LARGE = 24 * 1024 * 1024, 40 * 1024 * 1024
SMEM, VMEM = pl.BlockSpec(memory_space=pltpu.SMEM), pl.BlockSpec(memory_space=pltpu.VMEM)
ANY = pl.BlockSpec(memory_space=pl.ANY)


def xor_permute(value, axis, mask):
    count = lax.axis_size(axis)
    return lax.ppermute(value, axis, [(i, i ^ mask) for i in range(count)])


def call(body, outs, *args, specs=None, after=(), flag=False, cost=0, scratch=(), limit=VMEM_LIMIT):
    specs = specs or [VMEM] * len(args)
    moved = sum(a.size * a.dtype.itemsize for a in args)
    outs = list(outs) + [((8, 128), F32)] * flag

    def kernel(*refs):
        refs = list(refs[: len(args)] + refs[len(args) + len(after) :])
        if flag:
            ref = refs.pop(len(args) + len(outs) - 1)
            ref[...] = jnp.zeros(ref.shape, F32)
        body(*refs)

    return pl.pallas_call(
        kernel,
        out_shape=[jax.ShapeDtypeStruct(shape, dtype) for shape, dtype in outs],
        in_specs=specs + [VMEM] * len(after),
        out_specs=[VMEM] * len(outs),
        scratch_shapes=list(scratch),
        compiler_params=pltpu.CompilerParams(vmem_limit_bytes=limit),
        cost_estimate=pl.CostEstimate(flops=cost, bytes_accessed=moved, transcendentals=0),
    )(*args, *after)


SENT = ((1, 0), (2, 0), (3, 1), (2, 1))
KEPT = ((0, 0), (3, 0), (0, 1), (1, 1))


def fetch(here_ref, a_ref, held, sems, first, parts):
    order = SENT + KEPT
    rows = held.shape[0] // (len(parts) * len(order))
    copies = []
    for own, stream in parts:
        base = (here_ref[2] if own else 1 - here_ref[2]) * 16 + stream * 2
        for owner, part in order:
            start = (base + lax.bitwise_xor(here_ref[0], owner) * 4 + part) * rows
            to = held.at[pl.ds(rows * len(copies), rows), :]
            block = a_ref.at[pl.ds(pl.multiple_of(start, rows), rows), :]
            copies.append(pltpu.make_async_copy(block, to, sems.at[first + len(copies)]))
    for copy in copies:
        copy.start()
    return copies


def multiply(a_ref, b_ref, out_ref, at):
    rows = a_ref.shape[0] // 3
    out_ref[...] = jnp.dot(a_ref[at * rows : (at + 1) * rows, :], b_ref[...], preferred_element_type=F32)


def pack(ref, value):
    rows = value.shape[0]
    top = jnp.maximum(jnp.max(jnp.abs(value), axis=0, keepdims=True), 1e-30)
    level = jnp.clip(jnp.ceil(jnp.log2(top * (1.0 / 32000.0)) * 256.0), -32000.0, 32000.0)
    scaled = value * jnp.exp2(level * (-1.0 / 256.0))
    ref[:rows, :] = jnp.round(scaled).astype(jnp.int32).astype(I16)
    ref[rows:, :] = jnp.broadcast_to(level, (TAIL, value.shape[1])).astype(jnp.int32).astype(I16)


def unpack(ref):
    rows = ref.shape[0] - TAIL
    level = ref[rows:, :].astype(jnp.int32).astype(F32)[0:1, :]
    return ref[:rows, :].astype(jnp.int32).astype(F32) * jnp.exp2(level * (1.0 / 256.0))


def first_messages(own_ref, other_ref, kept_ref, a_ref, b_ref):
    rows = own_ref.shape[0] // 4
    pack(a_ref, own_ref[:rows, :] + other_ref[:rows, :])
    pack(b_ref, own_ref[rows : 2 * rows, :] + other_ref[rows : 2 * rows, :])
    kept_ref[...] = own_ref[2 * rows :, :] + other_ref[2 * rows : 4 * rows, :]


def second_messages(sum_ref, a_in, b_in, kept_ref, a_ref, b_ref):
    rows = sum_ref.shape[0] // 4
    for part, (came, out) in enumerate(((a_in, a_ref), (b_in, b_ref))):
        at = 2 * part * rows
        total = sum_ref[at : at + 2 * rows, :] + unpack(came)
        kept_ref[part * rows : (part + 1) * rows, :] = total[:rows, :]
        pack(out, total[rows:, :])


def split_four(mine, work_ref, own_ref, message_refs, masks):
    quarter = work_ref.shape[0] // 4

    def rows_of(owner):
        return work_ref[pl.ds(pl.multiple_of(owner * quarter, quarter), quarter), :]

    for mask, out in zip(masks, message_refs):
        pack(out, rows_of(lax.bitwise_xor(mine, mask)))
    own_ref[...] = rows_of(mine)


def third_messages(here_ref, kept_ref, a_in, b_in, own_ref, m1_ref, m2_ref, m3_ref, work_ref):
    half = kept_ref.shape[0] // 2
    work_ref[:half, :] = kept_ref[:half, :] + unpack(a_in)
    work_ref[half:, :] = kept_ref[half:, :] + unpack(b_in)
    split_four(here_ref[1], work_ref, own_ref, (m1_ref, m2_ref, m3_ref), Z_ORDER)


def last_sum(own_ref, m1_in, m2_in, m3_in, out_ref):
    out_ref[...] = (own_ref[...] + unpack(m1_in) + unpack(m2_in) + unpack(m3_in)).astype(BF16)


def join(p0_ref, p1_ref, p2_ref, p3_ref, out_ref):
    rows = p0_ref.shape[0]
    for i, ref in enumerate((p0_ref, p1_ref, p2_ref, p3_ref)):
        out_ref[rows * i : rows * (i + 1), :] = ref[...]


def gram_messages(here_ref, mine_ref, came_ref, own_ref, m1_ref, m2_ref, m3_ref, work_ref):
    work_ref[...] = mine_ref[...] + came_ref[...]
    split_four(here_ref[3] // 2, work_ref, own_ref, (m1_ref, m2_ref, m3_ref), Y_ORDER)


def gram_halves(here_ref, own_ref, m1_in, m2_in, m3_in, kept_ref, out_ref, work_ref):
    rows = kept_ref.shape[0]
    work_ref[...] = own_ref[...] + unpack(m1_in) + unpack(m2_in) + unpack(m3_in)
    half = here_ref[3] % 2
    kept_ref[...] = work_ref[pl.ds(pl.multiple_of(half * rows, rows), rows), :]
    pack(out_ref, work_ref[pl.ds(pl.multiple_of((1 - half) * rows, rows), rows), :])


def weights_kernel(here_ref, val_table, freq_ref, other_ref, ci_ref, vi_ref, ce_ref, *out_refs):
    shape = ci_ref.shape
    half = shape[1] // 2
    index = ci_ref[...]
    high, low = index // 128, index % 128
    cond = jnp.zeros(shape, F32)
    for row in range(ce_ref.shape[0]):
        table = jnp.broadcast_to(ce_ref[row : row + 1, :], shape)
        cond = jnp.where(high == row, jnp.take_along_axis(table, low, axis=1), cond)
    level = vi_ref[...]
    val = jnp.zeros(shape, F32)
    for row in range(val_table.shape[0]):
        val = jnp.where(level == row, val_table[row], val)
    spacing = cond - val
    swapped = jnp.concatenate([spacing[:, half:], spacing[:, :half]], axis=1)
    spacing = jnp.where(here_ref[1] % 2 == 1, swapped, spacing)
    for freq, out_ref in zip((freq_ref[0], other_ref[0:1, 0:1]), out_refs):
        out_ref[...] = 2.0 * spacing / (spacing * spacing + freq * freq)


def gram_step(here, weights, pieces, places, grams, extra=0):
    width = pieces[0].shape[1]
    count, kinds = len(pieces), len(weights)

    def body(here_ref, *refs):
        w_refs, came, before, out_refs = refs[:kinds], refs[kinds : kinds + count], refs[kinds + count : -kinds], refs[-kinds:]
        totals = [ref[...] for ref in before] or [None] * kinds
        for ref, (stream, owner) in zip(came, places):
            first = (here_ref[2] * 4 + lax.bitwise_xor(here_ref[0], owner)) * 4 + stream * 2
            parts = [[] for _ in range(kinds)]
            for j in range(2):
                rows = ref[128 * j : 128 * (j + 1), :].astype(F32).T
                for part, w_ref in zip(parts, w_refs):
                    w = w_ref[pl.ds(first + lax.bitwise_xor(here_ref[1] // 2, j), 1), :]
                    part.append((rows * w).astype(BF16))
            for kind, part in enumerate(parts):
                term = jnp.dot(jnp.concatenate(part, axis=1), ref[...], preferred_element_type=F32)
                totals[kind] = term if totals[kind] is None else totals[kind] + term
        for out_ref, total in zip(out_refs, totals):
            out_ref[...] = total

    return call(
        body,
        [((width, width), F32)] * kinds,
        here,
        *weights,
        *pieces,
        *grams,
        cost=2 * kinds * width * width * sum(p.shape[0] for p in pieces) + extra,
        specs=[SMEM] + [VMEM] * (kinds + count + len(grams)),
    )


def on_device(pair_elements, subspace, val_energy, cond_energy, val_index, cond_index, frequencies):
    here = jnp.stack([lax.axis_index(name).astype(jnp.int32) for name in PW + ("pair",)])
    rows, width = pair_elements.shape[0], subspace.shape[1]
    unit = rows // 64
    message = lambda count: ((count + TAIL, width), I16)
    sums = lambda count: ((count, width), F32)
    both = range(2)

    def first_other(here_ref, freq_ref, a_ref, b_ref, out_ref, held_ref, work_ref, sems):
        now = fetch(here_ref, a_ref, work_ref, sems, 0, [(False, 0)])
        later = fetch(here_ref, a_ref, held_ref, sems, 8, [(True, 0), (False, 1), (True, 1)])
        out_ref[16 * unit :, :] = jnp.full((8, width), freq_ref[0], F32)
        for copy in now:
            copy.wait()
        out_ref[: 16 * unit, :] = jnp.dot(work_ref[...], b_ref[...], preferred_element_type=F32)
        for copy in later:
            copy.wait()

    def first_own(a_ref, b_ref, own_ref, other_ref):
        multiply(a_ref, b_ref, own_ref, 0)
        multiply(a_ref, b_ref, other_ref, 1)

    def second_own(a_ref, b_ref, own_ref):
        multiply(a_ref, b_ref, own_ref, 2)

    kept, a, b = [None] * 2, [None] * 2, [None] * 2
    first = [sums(8 * unit)] + [message(4 * unit)] * 2
    depth = pair_elements.shape[1]
    cost = 2 * 16 * unit * depth * width
    other, held, done = call(
        first_other,
        [sums(16 * unit + 8), ((48 * unit, depth), BF16)],
        here,
        frequencies,
        pair_elements,
        subspace,
        specs=[SMEM, SMEM, ANY, VMEM],
        flag=True,
        cost=cost,
        scratch=[pltpu.VMEM((16 * unit, depth), BF16), pltpu.SemaphoreType.DMA((32,))],
        limit=VMEM_LARGE,
    )
    other_in = xor_permute(other, "pw_c", 1)
    own, other = call(first_own, [sums(16 * unit)] * 2, held, subspace, after=[done], cost=2 * cost)
    other, other_in = lax.optimization_barrier((other, other_in))
    kept[0], a[0], b[0], done = call(first_messages, first, own, other_in, flag=True)
    own = call(second_own, [sums(16 * unit)], held, subspace, after=[done], cost=cost)[0]
    kept[1], a[1], b[1] = call(first_messages, first, own, xor_permute(other, "pw_c", 1))

    last = None
    for s in both:
        a[s], b[s] = xor_permute(a[s], "pw_x", 1), xor_permute(b[s], "pw_x", 3)
    for s in both:
        after = [] if last is None else [last]
        kept[s], a[s], b[s], last = call(
            second_messages, [sums(4 * unit)] + [message(2 * unit)] * 2, kept[s], a[s], b[s], after=after, flag=True
        )
        a[s], b[s] = xor_permute(a[s], "pw_x", 3), xor_permute(b[s], "pw_x", 1)
    came = [None] * 2
    for s in both:
        own, *out, last = call(
            third_messages,
            [sums(unit)] + [message(unit)] * 3,
            here,
            kept[s],
            a[s],
            b[s],
            specs=[SMEM] + [VMEM] * 3,
            after=[last],
            flag=True,
            scratch=[pltpu.VMEM((4 * unit, width), F32)],
        )
        came[s] = [own] + [xor_permute(value, "pw_z", mask) for mask, value in zip(Z_ORDER, out)]
    weights = call(
        weights_kernel,
        [((rows // 128, 128), F32)] * 2,
        here,
        val_energy,
        frequencies,
        other_in[16 * unit :, :128],
        cond_index.reshape(-1, 128),
        val_index.reshape(-1, 128),
        cond_energy.reshape(-1, 128),
        specs=[SMEM] * 3 + [VMEM] * 4,
        after=[last],
    )

    last = weights[0]
    pieces = [None] * 2
    for s in both:
        own, last = call(last_sum, [((unit, width), BF16)], *came[s], after=[last], flag=True)
        pieces[s] = [own] + [xor_permute(own, "pw_z", mask) for mask in (1, 2, 3)]
    quarters, near, far = [None] * 2, [None] * 2, [None] * 2
    for s in both:
        quarters[s], last = call(join, [((4 * unit, width), BF16)], *pieces[s], after=[last], flag=True)
        near[s], far[s] = xor_permute(quarters[s], "pw_x", 1), xor_permute(quarters[s], "pw_x", 3)
        near[s], far[s] = lax.optimization_barrier((near[s], far[s]))
    grams = gram_step(here, weights, quarters, [(0, 0), (1, 0)], [], 3_000_000_000)
    near[0], far[0], grams = lax.optimization_barrier((near[0], far[0], grams))
    across = [xor_permute(far[0], "pw_x", 1), xor_permute(near[1], "pw_x", 3)]
    grams = gram_step(here, weights, [near[0], far[0]], [(0, 1), (0, 3)], grams)
    grams = gram_step(here, weights, [near[1], far[1], across[0]], [(1, 1), (1, 3), (0, 2)], grams)
    mine, theirs = gram_step(here, weights, [across[1]], [(1, 2)], grams)

    part = width // 4
    own, *out = call(
        gram_messages,
        [sums(part)] + [message(part)] * 3,
        here,
        mine,
        xor_permute(theirs, "pw_c", 1),
        specs=[SMEM] + [VMEM] * 2,
        scratch=[pltpu.VMEM((width, width), F32)],
    )
    came = [xor_permute(value, "pair", 2 * mask) for mask, value in zip(Y_ORDER, out)]
    own, out = call(
        gram_halves,
        [sums(part // 2), message(part // 2)],
        here,
        own,
        *came,
        specs=[SMEM] + [VMEM] * 4,
        scratch=[pltpu.VMEM((part, width), F32)],
    )
    factor = -4.0 / (rows * lax.axis_size("pair"))

    def finish(own_ref, came_ref, out_ref):
        out_ref[...] = (own_ref[...] + unpack(came_ref)) * factor

    return call(finish, [sums(part // 2)], own, xor_permute(out, "pair", 1))[0][None]


def solution(mesh):
    torus = Mesh(mesh.devices.reshape(mesh.shape["pair"], 4, 4, 2), ("pair",) + PW)
    return jax.shard_map(
        on_device,
        mesh=torus,
        in_specs=(P("pair", PW), P(PW, None), P(), P(), P("pair"), P("pair"), P(PW)),
        out_specs=P(PW, "pair", None),
        check_vma=False,
    )
```

```python
import jax
import jax.numpy as jnp
from jax import lax
from jax.experimental import pallas as pl
from jax.experimental.pallas import tpu as pltpu
from jax.sharding import Mesh
from jax.sharding import PartitionSpec as P

PW = ("pw_x", "pw_z", "pw_c")
F32, BF16, I16 = jnp.float32, jnp.bfloat16, jnp.int16
TAIL = 16
Z_ORDER, Y_ORDER = (3, 2, 1), (2, 3, 1)
VMEM_LIMIT, VMEM_LARGE = 24 * 1024 * 1024, 40 * 1024 * 1024
SMEM, VMEM = pl.BlockSpec(memory_space=pltpu.SMEM), pl.BlockSpec(memory_space=pltpu.VMEM)
ANY = pl.BlockSpec(memory_space=pl.ANY)


def xor_permute(value, axis, mask):
    count = lax.axis_size(axis)
    return lax.ppermute(value, axis, [(i, i ^ mask) for i in range(count)])


def call(body, outs, *args, specs=None, after=(), flag=False, cost=0, scratch=(), limit=VMEM_LIMIT):
    specs = specs or [VMEM] * len(args)
    moved = sum(a.size * a.dtype.itemsize for a in args)
    outs = list(outs) + [((8, 128), F32)] * flag

    def kernel(*refs):
        refs = list(refs[: len(args)] + refs[len(args) + len(after) :])
        if flag:
            ref = refs.pop(len(args) + len(outs) - 1)
            ref[...] = jnp.zeros(ref.shape, F32)
        body(*refs)

    return pl.pallas_call(
        kernel,
        out_shape=[jax.ShapeDtypeStruct(shape, dtype) for shape, dtype in outs],
        in_specs=specs + [VMEM] * len(after),
        out_specs=[VMEM] * len(outs),
        scratch_shapes=list(scratch),
        compiler_params=pltpu.CompilerParams(vmem_limit_bytes=limit),
        cost_estimate=pl.CostEstimate(flops=cost, bytes_accessed=moved, transcendentals=0),
    )(*args, *after)


SENT = ((1, 0), (2, 0), (3, 1), (2, 1))
KEPT = ((0, 0), (3, 0), (0, 1), (1, 1))


def fetch(here_ref, a_ref, held, sems, first, parts):
    order = SENT + KEPT
    rows = held.shape[0] // (len(parts) * len(order))
    copies = []
    for own, stream in parts:
        base = (here_ref[2] if own else 1 - here_ref[2]) * 16 + stream * 2
        for owner, part in order:
            start = (base + lax.bitwise_xor(here_ref[0], owner) * 4 + part) * rows
            to = held.at[pl.ds(rows * len(copies), rows), :]
            block = a_ref.at[pl.ds(pl.multiple_of(start, rows), rows), :]
            copies.append(pltpu.make_async_copy(block, to, sems.at[first + len(copies)]))
    for copy in copies:
        copy.start()
    return copies


def multiply(a_ref, b_ref, out_ref, at):
    rows = a_ref.shape[0] // 3
    out_ref[...] = jnp.dot(a_ref[at * rows : (at + 1) * rows, :], b_ref[...], preferred_element_type=F32)


def pack(ref, value):
    rows = value.shape[0]
    top = jnp.maximum(jnp.max(jnp.abs(value), axis=0, keepdims=True), 1e-30)
    level = jnp.clip(jnp.ceil(jnp.log2(top * (1.0 / 32000.0)) * 256.0), -32000.0, 32000.0)
    scaled = value * jnp.exp2(level * (-1.0 / 256.0))
    ref[:rows, :] = jnp.round(scaled).astype(jnp.int32).astype(I16)
    ref[rows:, :] = jnp.broadcast_to(level, (TAIL, value.shape[1])).astype(jnp.int32).astype(I16)


def unpack(ref):
    rows = ref.shape[0] - TAIL
    level = ref[rows:, :].astype(jnp.int32).astype(F32)[0:1, :]
    return ref[:rows, :].astype(jnp.int32).astype(F32) * jnp.exp2(level * (1.0 / 256.0))


def first_messages(own_ref, other_ref, kept_ref, a_ref, b_ref):
    rows = own_ref.shape[0] // 4
    pack(a_ref, own_ref[:rows, :] + other_ref[:rows, :])
    pack(b_ref, own_ref[rows : 2 * rows, :] + other_ref[rows : 2 * rows, :])
    kept_ref[...] = own_ref[2 * rows :, :] + other_ref[2 * rows : 4 * rows, :]


def second_messages(sum_ref, a_in, b_in, kept_ref, a_ref, b_ref):
    rows = sum_ref.shape[0] // 4
    for part, (came, out) in enumerate(((a_in, a_ref), (b_in, b_ref))):
        at = 2 * part * rows
        total = sum_ref[at : at + 2 * rows, :] + unpack(came)
        kept_ref[part * rows : (part + 1) * rows, :] = total[:rows, :]
        pack(out, total[rows:, :])


def split_four(mine, work_ref, own_ref, message_refs, masks):
    quarter = work_ref.shape[0] // 4

    def rows_of(owner):
        return work_ref[pl.ds(pl.multiple_of(owner * quarter, quarter), quarter), :]

    for mask, out in zip(masks, message_refs):
        pack(out, rows_of(lax.bitwise_xor(mine, mask)))
    own_ref[...] = rows_of(mine)


def third_messages(here_ref, kept_ref, a_in, b_in, own_ref, m1_ref, m2_ref, m3_ref, work_ref):
    half = kept_ref.shape[0] // 2
    work_ref[:half, :] = kept_ref[:half, :] + unpack(a_in)
    work_ref[half:, :] = kept_ref[half:, :] + unpack(b_in)
    split_four(here_ref[1], work_ref, own_ref, (m1_ref, m2_ref, m3_ref), Z_ORDER)


def last_sum(own_ref, m1_in, m2_in, m3_in, out_ref):
    out_ref[...] = (own_ref[...] + unpack(m1_in) + unpack(m2_in) + unpack(m3_in)).astype(BF16)


def join(first_ref, second_ref, out_ref):
    rows = first_ref.shape[0]
    out_ref[:rows, :] = first_ref[...]
    out_ref[rows:, :] = second_ref[...]


def gram_messages(here_ref, mine_ref, came_ref, own_ref, m1_ref, m2_ref, m3_ref, work_ref):
    work_ref[...] = mine_ref[...] + came_ref[...]
    split_four(here_ref[3] // 2, work_ref, own_ref, (m1_ref, m2_ref, m3_ref), Y_ORDER)


def gram_halves(here_ref, own_ref, m1_in, m2_in, m3_in, kept_ref, out_ref, work_ref):
    rows = kept_ref.shape[0]
    work_ref[...] = own_ref[...] + unpack(m1_in) + unpack(m2_in) + unpack(m3_in)
    half = here_ref[3] % 2
    kept_ref[...] = work_ref[pl.ds(pl.multiple_of(half * rows, rows), rows), :]
    pack(out_ref, work_ref[pl.ds(pl.multiple_of((1 - half) * rows, rows), rows), :])


def weights_kernel(here_ref, val_table, freq_ref, other_ref, ci_ref, vi_ref, ce_ref, *out_refs):
    shape = ci_ref.shape
    half = shape[1] // 2
    index = ci_ref[...]
    high, low = index // 128, index % 128
    cond = jnp.zeros(shape, F32)
    for row in range(ce_ref.shape[0]):
        table = jnp.broadcast_to(ce_ref[row : row + 1, :], shape)
        cond = jnp.where(high == row, jnp.take_along_axis(table, low, axis=1), cond)
    level = vi_ref[...]
    val = jnp.zeros(shape, F32)
    for row in range(val_table.shape[0]):
        val = jnp.where(level == row, val_table[row], val)
    spacing = cond - val
    swapped = jnp.concatenate([spacing[:, half:], spacing[:, :half]], axis=1)
    spacing = jnp.where(here_ref[1] % 2 == 1, swapped, spacing)
    for freq, out_ref in zip((freq_ref[0], other_ref[0:1, 0:1]), out_refs):
        out_ref[...] = 2.0 * spacing / (spacing * spacing + freq * freq)


def gram_step(here, weights, pieces, places, grams, extra=0):
    width = pieces[0].shape[1]
    count, kinds = len(pieces), len(weights)

    def body(here_ref, *refs):
        w_refs, came, before, out_refs = refs[:kinds], refs[kinds : kinds + count], refs[kinds + count : -kinds], refs[-kinds:]
        totals = [ref[...] for ref in before] or [None] * kinds
        for ref, (stream, owner, core) in zip(came, places):
            first = (lax.bitwise_xor(here_ref[2], core) * 4 + lax.bitwise_xor(here_ref[0], owner)) * 4 + stream * 2
            parts = [[] for _ in range(kinds)]
            for j in range(2):
                rows = ref[128 * j : 128 * (j + 1), :].astype(F32).T
                for part, w_ref in zip(parts, w_refs):
                    w = w_ref[pl.ds(first + lax.bitwise_xor(here_ref[1] // 2, j), 1), :]
                    part.append((rows * w).astype(BF16))
            for kind, part in enumerate(parts):
                term = jnp.dot(jnp.concatenate(part, axis=1), ref[...], preferred_element_type=F32)
                totals[kind] = term if totals[kind] is None else totals[kind] + term
        for out_ref, total in zip(out_refs, totals):
            out_ref[...] = total

    return call(
        body,
        [((width, width), F32)] * kinds,
        here,
        *weights,
        *pieces,
        *grams,
        cost=2 * kinds * width * width * sum(p.shape[0] for p in pieces) + extra,
        specs=[SMEM] + [VMEM] * (kinds + count + len(grams)),
    )


def on_device(pair_elements, subspace, val_energy, cond_energy, val_index, cond_index, frequencies):
    here = jnp.stack([lax.axis_index(name).astype(jnp.int32) for name in PW + ("pair",)])
    rows, width = pair_elements.shape[0], subspace.shape[1]
    unit = rows // 64
    message = lambda count: ((count + TAIL, width), I16)
    sums = lambda count: ((count, width), F32)
    both = range(2)

    def first_other(here_ref, freq_ref, a_ref, b_ref, out_ref, held_ref, work_ref, sems):
        now = fetch(here_ref, a_ref, work_ref, sems, 0, [(False, 0)])
        later = fetch(here_ref, a_ref, held_ref, sems, 8, [(True, 0), (False, 1), (True, 1)])
        out_ref[16 * unit :, :] = jnp.full((8, width), freq_ref[0], F32)
        for copy in now:
            copy.wait()
        out_ref[: 16 * unit, :] = jnp.dot(work_ref[...], b_ref[...], preferred_element_type=F32)
        for copy in later:
            copy.wait()

    def first_own(a_ref, b_ref, own_ref, other_ref):
        multiply(a_ref, b_ref, own_ref, 0)
        multiply(a_ref, b_ref, other_ref, 1)

    def second_own(a_ref, b_ref, own_ref):
        multiply(a_ref, b_ref, own_ref, 2)

    kept, a, b = [None] * 2, [None] * 2, [None] * 2
    first = [sums(8 * unit)] + [message(4 * unit)] * 2
    depth = pair_elements.shape[1]
    cost = 2 * 16 * unit * depth * width
    other, held, done = call(
        first_other,
        [sums(16 * unit + 8), ((48 * unit, depth), BF16)],
        here,
        frequencies,
        pair_elements,
        subspace,
        specs=[SMEM, SMEM, ANY, VMEM],
        flag=True,
        cost=cost,
        scratch=[pltpu.VMEM((16 * unit, depth), BF16), pltpu.SemaphoreType.DMA((32,))],
        limit=VMEM_LARGE,
    )
    other_in = xor_permute(other, "pw_c", 1)
    own, other = call(first_own, [sums(16 * unit)] * 2, held, subspace, after=[done], cost=2 * cost)
    other, other_in = lax.optimization_barrier((other, other_in))
    kept[0], a[0], b[0], done = call(first_messages, first, own, other_in, flag=True)
    own = call(second_own, [sums(16 * unit)], held, subspace, after=[done], cost=cost)[0]
    kept[1], a[1], b[1] = call(first_messages, first, own, xor_permute(other, "pw_c", 1))

    last = None
    for s in both:
        a[s], b[s] = xor_permute(a[s], "pw_x", 1), xor_permute(b[s], "pw_x", 3)
    for s in both:
        after = [] if last is None else [last]
        kept[s], a[s], b[s], last = call(
            second_messages, [sums(4 * unit)] + [message(2 * unit)] * 2, kept[s], a[s], b[s], after=after, flag=True
        )
        a[s], b[s] = xor_permute(a[s], "pw_x", 3), xor_permute(b[s], "pw_x", 1)
    came = [None] * 2
    for s in both:
        own, *out, last = call(
            third_messages,
            [sums(unit)] + [message(unit)] * 3,
            here,
            kept[s],
            a[s],
            b[s],
            specs=[SMEM] + [VMEM] * 3,
            after=[last],
            flag=True,
            scratch=[pltpu.VMEM((4 * unit, width), F32)],
        )
        came[s] = [own] + [xor_permute(value, "pw_z", mask) for mask, value in zip(Z_ORDER, out)]
    weights = call(
        weights_kernel,
        [((rows // 128, 128), F32)] * 2,
        here,
        val_energy,
        frequencies,
        other_in[16 * unit :, :128],
        cond_index.reshape(-1, 128),
        val_index.reshape(-1, 128),
        cond_energy.reshape(-1, 128),
        specs=[SMEM] * 3 + [VMEM] * 4,
        after=[last],
    )

    last = weights[0]
    pieces, near, far, quarters = [None] * 2, [None] * 2, [None] * 2, [None] * 2
    for s in both:
        own, last = call(last_sum, [((unit, width), BF16)], *came[s], after=[last], flag=True)
        pieces[s] = own, xor_permute(own, "pw_z", 1)
    for s in both:
        own, last = call(join, [((2 * unit, width), BF16)], *pieces[s], after=[last], flag=True)
        pieces[s] = own, xor_permute(own, "pw_z", 2)
    for s in both:
        quarters[s], last = call(join, [((4 * unit, width), BF16)], *pieces[s], after=[last], flag=True)
        near[s], far[s] = xor_permute(quarters[s], "pw_x", 1), xor_permute(quarters[s], "pw_x", 3)
        near[s], far[s] = lax.optimization_barrier((near[s], far[s]))
    grams = gram_step(here, weights, quarters, [(0, 0, 0), (1, 0, 0)], [], 3_000_000_000)
    near[0], far[0], grams = lax.optimization_barrier((near[0], far[0], grams))
    across = [xor_permute(far[0], "pw_x", 1), xor_permute(near[1], "pw_x", 3)]
    grams = gram_step(here, weights, [near[0], far[0]], [(0, 1, 0), (0, 3, 0)], grams)
    grams = gram_step(here, weights, [near[1], far[1], across[0]], [(1, 1, 0), (1, 3, 0), (0, 2, 0)], grams)
    mine, theirs = grams
    theirs = xor_permute(theirs, "pw_c", 1)
    other = xor_permute(across[1], "pw_c", 1)
    mine = gram_step(here, weights[:1], [across[1]], [(1, 2, 0)], [mine], 4_000_000_000)
    mine = gram_step(here, weights[:1], [other], [(1, 2, 1)], mine, 5_000_000_000)[0]

    part = width // 4
    own, *out = call(
        gram_messages,
        [sums(part)] + [message(part)] * 3,
        here,
        mine,
        theirs,
        specs=[SMEM] + [VMEM] * 2,
        scratch=[pltpu.VMEM((width, width), F32)],
    )
    came = [xor_permute(value, "pair", 2 * mask) for mask, value in zip(Y_ORDER, out)]
    own, out = call(
        gram_halves,
        [sums(part // 2), message(part // 2)],
        here,
        own,
        *came,
        specs=[SMEM] + [VMEM] * 4,
        scratch=[pltpu.VMEM((part, width), F32)],
    )
    factor = -4.0 / (rows * lax.axis_size("pair"))

    def finish(own_ref, came_ref, out_ref):
        out_ref[...] = (own_ref[...] + unpack(came_ref)) * factor

    return call(finish, [sums(part // 2)], own, xor_permute(out, "pair", 1))[0][None]


def solution(mesh):
    torus = Mesh(mesh.devices.reshape(mesh.shape["pair"], 4, 4, 2), ("pair",) + PW)
    return jax.shard_map(
        on_device,
        mesh=torus,
        in_specs=(P("pair", PW), P(PW, None), P(), P(), P("pair"), P("pair"), P(PW)),
        out_specs=P(PW, "pair", None),
        check_vma=False,
    )
```

```python
import jax
import jax.numpy as jnp
from jax import lax
from jax.experimental import pallas as pl
from jax.experimental.pallas import tpu as pltpu
from jax.sharding import Mesh
from jax.sharding import PartitionSpec as P

PW = ("pw_x", "pw_z", "pw_c")
F32, BF16, I16 = jnp.float32, jnp.bfloat16, jnp.int16
TAIL = 16
Z_ORDER, Y_ORDER = (3, 2, 1), (2, 3, 1)
VMEM_LIMIT, VMEM_LARGE = 24 * 1024 * 1024, 40 * 1024 * 1024
SMEM, VMEM = pl.BlockSpec(memory_space=pltpu.SMEM), pl.BlockSpec(memory_space=pltpu.VMEM)
ANY = pl.BlockSpec(memory_space=pl.ANY)


def xor_permute(value, axis, mask):
    count = lax.axis_size(axis)
    return lax.ppermute(value, axis, [(i, i ^ mask) for i in range(count)])


def call(body, outs, *args, specs=None, after=(), flag=False, cost=0, scratch=(), limit=VMEM_LIMIT):
    specs = specs or [VMEM] * len(args)
    moved = sum(a.size * a.dtype.itemsize for a in args)
    outs = list(outs) + [((8, 128), F32)] * flag

    def kernel(*refs):
        refs = list(refs[: len(args)] + refs[len(args) + len(after) :])
        if flag:
            ref = refs.pop(len(args) + len(outs) - 1)
            ref[...] = jnp.zeros(ref.shape, F32)
        body(*refs)

    return pl.pallas_call(
        kernel,
        out_shape=[jax.ShapeDtypeStruct(shape, dtype) for shape, dtype in outs],
        in_specs=specs + [VMEM] * len(after),
        out_specs=[VMEM] * len(outs),
        scratch_shapes=list(scratch),
        compiler_params=pltpu.CompilerParams(vmem_limit_bytes=limit),
        cost_estimate=pl.CostEstimate(flops=cost, bytes_accessed=moved, transcendentals=0),
    )(*args, *after)


SENT = ((1, 0), (2, 0), (3, 1), (2, 1))
KEPT = ((0, 0), (3, 0), (0, 1), (1, 1))


def fetch(here_ref, a_ref, held, sems, first, parts):
    order = SENT + KEPT
    rows = held.shape[0] // (len(parts) * len(order))
    copies = []
    for own, stream in parts:
        base = (here_ref[2] if own else 1 - here_ref[2]) * 16 + stream * 2
        for owner, part in order:
            start = (base + lax.bitwise_xor(here_ref[0], owner) * 4 + part) * rows
            to = held.at[pl.ds(rows * len(copies), rows), :]
            block = a_ref.at[pl.ds(pl.multiple_of(start, rows), rows), :]
            copies.append(pltpu.make_async_copy(block, to, sems.at[first + len(copies)]))
    for copy in copies:
        copy.start()
    return copies


def multiply(a_ref, b_ref, out_ref, at):
    rows = a_ref.shape[0] // 3
    out_ref[...] = jnp.dot(a_ref[at * rows : (at + 1) * rows, :], b_ref[...], preferred_element_type=F32)


def pack(ref, value):
    rows = value.shape[0]
    top = jnp.maximum(jnp.max(jnp.abs(value), axis=0, keepdims=True), 1e-30)
    level = jnp.clip(jnp.ceil(jnp.log2(top * (1.0 / 32000.0)) * 256.0), -32000.0, 32000.0)
    scaled = value * jnp.exp2(level * (-1.0 / 256.0))
    ref[:rows, :] = jnp.round(scaled).astype(jnp.int32).astype(I16)
    ref[rows:, :] = jnp.broadcast_to(level, (TAIL, value.shape[1])).astype(jnp.int32).astype(I16)


def unpack(ref):
    rows = ref.shape[0] - TAIL
    level = ref[rows:, :].astype(jnp.int32).astype(F32)[0:1, :]
    return ref[:rows, :].astype(jnp.int32).astype(F32) * jnp.exp2(level * (1.0 / 256.0))


def first_messages(own_ref, other_ref, kept_ref, a_ref, b_ref):
    rows = own_ref.shape[0] // 4
    pack(a_ref, own_ref[:rows, :] + other_ref[:rows, :])
    pack(b_ref, own_ref[rows : 2 * rows, :] + other_ref[rows : 2 * rows, :])
    kept_ref[...] = own_ref[2 * rows :, :] + other_ref[2 * rows : 4 * rows, :]


def second_messages(sum_ref, a_in, b_in, kept_ref, a_ref, b_ref):
    rows = sum_ref.shape[0] // 4
    for part, (came, out) in enumerate(((a_in, a_ref), (b_in, b_ref))):
        at = 2 * part * rows
        total = sum_ref[at : at + 2 * rows, :] + unpack(came)
        kept_ref[part * rows : (part + 1) * rows, :] = total[:rows, :]
        pack(out, total[rows:, :])


def split_four(mine, work_ref, own_ref, message_refs, masks):
    quarter = work_ref.shape[0] // 4

    def rows_of(owner):
        return work_ref[pl.ds(pl.multiple_of(owner * quarter, quarter), quarter), :]

    for mask, out in zip(masks, message_refs):
        pack(out, rows_of(lax.bitwise_xor(mine, mask)))
    own_ref[...] = rows_of(mine)


def third_messages(here_ref, kept_ref, a_in, b_in, own_ref, m1_ref, m2_ref, m3_ref, work_ref):
    half = kept_ref.shape[0] // 2
    work_ref[:half, :] = kept_ref[:half, :] + unpack(a_in)
    work_ref[half:, :] = kept_ref[half:, :] + unpack(b_in)
    split_four(here_ref[1], work_ref, own_ref, (m1_ref, m2_ref, m3_ref), Z_ORDER)


def last_sum(own_ref, m1_in, m2_in, m3_in, out_ref):
    out_ref[...] = (own_ref[...] + unpack(m1_in) + unpack(m2_in) + unpack(m3_in)).astype(BF16)


def join(p0_ref, p1_ref, p2_ref, p3_ref, out_ref):
    rows = p0_ref.shape[0]
    for i, ref in enumerate((p0_ref, p1_ref, p2_ref, p3_ref)):
        out_ref[rows * i : rows * (i + 1), :] = ref[...]


def gram_messages(here_ref, mine_ref, came_ref, own_ref, m1_ref, m2_ref, m3_ref, work_ref):
    work_ref[...] = mine_ref[...] + came_ref[...]
    split_four(here_ref[3] // 2, work_ref, own_ref, (m1_ref, m2_ref, m3_ref), Y_ORDER)


def gram_halves(here_ref, own_ref, m1_in, m2_in, m3_in, kept_ref, out_ref, work_ref):
    rows = kept_ref.shape[0]
    work_ref[...] = own_ref[...] + unpack(m1_in) + unpack(m2_in) + unpack(m3_in)
    half = here_ref[3] % 2
    kept_ref[...] = work_ref[pl.ds(pl.multiple_of(half * rows, rows), rows), :]
    pack(out_ref, work_ref[pl.ds(pl.multiple_of((1 - half) * rows, rows), rows), :])


def weights_kernel(here_ref, val_table, freq_ref, other_ref, ci_ref, vi_ref, ce_ref, *out_refs):
    shape = ci_ref.shape
    half = shape[1] // 2
    index = ci_ref[...]
    high, low = index // 128, index % 128
    cond = jnp.zeros(shape, F32)
    for row in range(ce_ref.shape[0]):
        table = jnp.broadcast_to(ce_ref[row : row + 1, :], shape)
        cond = jnp.where(high == row, jnp.take_along_axis(table, low, axis=1), cond)
    level = vi_ref[...]
    val = jnp.zeros(shape, F32)
    for row in range(val_table.shape[0]):
        val = jnp.where(level == row, val_table[row], val)
    spacing = cond - val
    swapped = jnp.concatenate([spacing[:, half:], spacing[:, :half]], axis=1)
    spacing = jnp.where(here_ref[1] % 2 == 1, swapped, spacing)
    for freq, out_ref in zip((freq_ref[0], other_ref[0:1, 0:1]), out_refs):
        out_ref[...] = 2.0 * spacing / (spacing * spacing + freq * freq)


def gram_step(here, weights, pieces, places, grams, extra=0):
    width = pieces[0].shape[1]
    count, kinds = len(pieces), len(weights)

    def body(here_ref, *refs):
        w_refs, came, before, out_refs = refs[:kinds], refs[kinds : kinds + count], refs[kinds + count : -kinds], refs[-kinds:]
        totals = [ref[...] for ref in before] or [None] * kinds
        for ref, (stream, owner, core) in zip(came, places):
            first = (lax.bitwise_xor(here_ref[2], core) * 4 + lax.bitwise_xor(here_ref[0], owner)) * 4 + stream * 2
            parts = [[] for _ in range(kinds)]
            for j in range(2):
                rows = ref[128 * j : 128 * (j + 1), :].astype(F32).T
                for part, w_ref in zip(parts, w_refs):
                    w = w_ref[pl.ds(first + lax.bitwise_xor(here_ref[1] // 2, j), 1), :]
                    part.append((rows * w).astype(BF16))
            for kind, part in enumerate(parts):
                term = jnp.dot(jnp.concatenate(part, axis=1), ref[...], preferred_element_type=F32)
                totals[kind] = term if totals[kind] is None else totals[kind] + term
        for out_ref, total in zip(out_refs, totals):
            out_ref[...] = total

    return call(
        body,
        [((width, width), F32)] * kinds,
        here,
        *weights,
        *pieces,
        *grams,
        cost=2 * kinds * width * width * sum(p.shape[0] for p in pieces) + extra,
        specs=[SMEM] + [VMEM] * (kinds + count + len(grams)),
    )


def on_device(pair_elements, subspace, val_energy, cond_energy, val_index, cond_index, frequencies):
    here = jnp.stack([lax.axis_index(name).astype(jnp.int32) for name in PW + ("pair",)])
    rows, width = pair_elements.shape[0], subspace.shape[1]
    unit = rows // 64
    message = lambda count: ((count + TAIL, width), I16)
    sums = lambda count: ((count, width), F32)
    both = range(2)

    def first_other(here_ref, freq_ref, a_ref, b_ref, out_ref, held_ref, work_ref, sems):
        now = fetch(here_ref, a_ref, work_ref, sems, 0, [(False, 0)])
        later = fetch(here_ref, a_ref, held_ref, sems, 8, [(True, 0), (False, 1), (True, 1)])
        out_ref[16 * unit :, :] = jnp.full((8, width), freq_ref[0], F32)
        for copy in now:
            copy.wait()
        out_ref[: 16 * unit, :] = jnp.dot(work_ref[...], b_ref[...], preferred_element_type=F32)
        for copy in later:
            copy.wait()

    def first_own(a_ref, b_ref, own_ref, other_ref):
        multiply(a_ref, b_ref, own_ref, 0)
        multiply(a_ref, b_ref, other_ref, 1)

    def second_own(a_ref, b_ref, own_ref):
        multiply(a_ref, b_ref, own_ref, 2)

    kept, a, b = [None] * 2, [None] * 2, [None] * 2
    first = [sums(8 * unit)] + [message(4 * unit)] * 2
    depth = pair_elements.shape[1]
    cost = 2 * 16 * unit * depth * width
    other, held, done = call(
        first_other,
        [sums(16 * unit + 8), ((48 * unit, depth), BF16)],
        here,
        frequencies,
        pair_elements,
        subspace,
        specs=[SMEM, SMEM, ANY, VMEM],
        flag=True,
        cost=cost,
        scratch=[pltpu.VMEM((16 * unit, depth), BF16), pltpu.SemaphoreType.DMA((32,))],
        limit=VMEM_LARGE,
    )
    other_in = xor_permute(other, "pw_c", 1)
    own, other = call(first_own, [sums(16 * unit)] * 2, held, subspace, after=[done], cost=2 * cost)
    other, other_in = lax.optimization_barrier((other, other_in))
    kept[0], a[0], b[0], done = call(first_messages, first, own, other_in, flag=True)
    own = call(second_own, [sums(16 * unit)], held, subspace, after=[done], cost=cost)[0]
    kept[1], a[1], b[1] = call(first_messages, first, own, xor_permute(other, "pw_c", 1))

    last = None
    for s in both:
        a[s], b[s] = xor_permute(a[s], "pw_x", 1), xor_permute(b[s], "pw_x", 3)
    for s in both:
        after = [] if last is None else [last]
        kept[s], a[s], b[s], last = call(
            second_messages, [sums(4 * unit)] + [message(2 * unit)] * 2, kept[s], a[s], b[s], after=after, flag=True
        )
        a[s], b[s] = xor_permute(a[s], "pw_x", 3), xor_permute(b[s], "pw_x", 1)
    came = [None] * 2
    for s in both:
        own, *out, last = call(
            third_messages,
            [sums(unit)] + [message(unit)] * 3,
            here,
            kept[s],
            a[s],
            b[s],
            specs=[SMEM] + [VMEM] * 3,
            after=[last],
            flag=True,
            scratch=[pltpu.VMEM((4 * unit, width), F32)],
        )
        came[s] = [own] + [xor_permute(value, "pw_z", mask) for mask, value in zip(Z_ORDER, out)]
    weights = call(
        weights_kernel,
        [((rows // 128, 128), F32)] * 2,
        here,
        val_energy,
        frequencies,
        other_in[16 * unit :, :128],
        cond_index.reshape(-1, 128),
        val_index.reshape(-1, 128),
        cond_energy.reshape(-1, 128),
        specs=[SMEM] * 3 + [VMEM] * 4,
        after=[last],
    )

    last = weights[0]
    pieces = [None] * 2
    for s in both:
        own, last = call(last_sum, [((unit, width), BF16)], *came[s], after=[last], flag=True)
        pieces[s] = [own] + [xor_permute(own, "pw_z", mask) for mask in (1, 2, 3)]
    quarters, near, far = [None] * 2, [None] * 2, [None] * 2
    last = [last]
    for s in both:
        quarters[s], *last = call(join, [((4 * unit, width), BF16)], *pieces[s], after=last, flag=s == 0)
        near[s], far[s] = xor_permute(quarters[s], "pw_x", 1), xor_permute(quarters[s], "pw_x", 3)
        near[s], far[s] = lax.optimization_barrier((near[s], far[s]))
    grams = gram_step(here, weights, quarters, [(0, 0, 0), (1, 0, 0)], [], 3_000_000_000)
    near[0], far[0], grams = lax.optimization_barrier((near[0], far[0], grams))
    across = [xor_permute(far[0], "pw_x", 1), xor_permute(near[1], "pw_x", 3)]
    grams = gram_step(here, weights, [near[0], far[0]], [(0, 1, 0), (0, 3, 0)], grams)
    grams = gram_step(here, weights, [near[1], far[1], across[0]], [(1, 1, 0), (1, 3, 0), (0, 2, 0)], grams)
    mine, theirs = grams
    theirs = xor_permute(theirs, "pw_c", 1)
    other = xor_permute(across[1], "pw_c", 1)
    mine = gram_step(here, weights[:1], [across[1]], [(1, 2, 0)], [mine], 4_000_000_000)
    mine = gram_step(here, weights[:1], [other], [(1, 2, 1)], mine, 5_000_000_000)[0]

    part = width // 4
    own, *out = call(
        gram_messages,
        [sums(part)] + [message(part)] * 3,
        here,
        mine,
        theirs,
        specs=[SMEM] + [VMEM] * 2,
        scratch=[pltpu.VMEM((width, width), F32)],
    )
    came = [xor_permute(value, "pair", 2 * mask) for mask, value in zip(Y_ORDER, out)]
    own, out = call(
        gram_halves,
        [sums(part // 2), message(part // 2)],
        here,
        own,
        *came,
        specs=[SMEM] + [VMEM] * 4,
        scratch=[pltpu.VMEM((part, width), F32)],
    )
    factor = -4.0 / (rows * lax.axis_size("pair"))

    def finish(own_ref, came_ref, out_ref):
        out_ref[...] = (own_ref[...] + unpack(came_ref)) * factor

    return call(finish, [sums(part // 2)], own, xor_permute(out, "pair", 1))[0][None]


def solution(mesh):
    torus = Mesh(mesh.devices.reshape(mesh.shape["pair"], 4, 4, 2), ("pair",) + PW)
    return jax.shard_map(
        on_device,
        mesh=torus,
        in_specs=(P("pair", PW), P(PW, None), P(), P(), P("pair"), P("pair"), P(PW)),
        out_specs=P(PW, "pair", None),
        check_vma=False,
    )
```

```python
import jax
import jax.numpy as jnp
from jax import lax
from jax.experimental import pallas as pl
from jax.experimental.pallas import tpu as pltpu
from jax.sharding import Mesh
from jax.sharding import PartitionSpec as P

PW = ("pw_x", "pw_z", "pw_c")
F32, BF16, I16 = jnp.float32, jnp.bfloat16, jnp.int16
TAIL = 16
Z_ORDER, Y_ORDER = (3, 2, 1), (2, 3, 1)
VMEM_LIMIT, VMEM_LARGE = 24 * 1024 * 1024, 40 * 1024 * 1024
SMEM, VMEM = pl.BlockSpec(memory_space=pltpu.SMEM), pl.BlockSpec(memory_space=pltpu.VMEM)
ANY = pl.BlockSpec(memory_space=pl.ANY)


def xor_permute(value, axis, mask):
    count = lax.axis_size(axis)
    return lax.ppermute(value, axis, [(i, i ^ mask) for i in range(count)])


def call(body, outs, *args, specs=None, after=(), flag=False, cost=0, scratch=(), limit=VMEM_LIMIT):
    specs = specs or [VMEM] * len(args)
    moved = sum(a.size * a.dtype.itemsize for a in args)
    outs = list(outs) + [((8, 128), F32)] * flag

    def kernel(*refs):
        refs = list(refs[: len(args)] + refs[len(args) + len(after) :])
        if flag:
            ref = refs.pop(len(args) + len(outs) - 1)
            ref[...] = jnp.zeros(ref.shape, F32)
        body(*refs)

    return pl.pallas_call(
        kernel,
        out_shape=[jax.ShapeDtypeStruct(shape, dtype) for shape, dtype in outs],
        in_specs=specs + [VMEM] * len(after),
        out_specs=[VMEM] * len(outs),
        scratch_shapes=list(scratch),
        compiler_params=pltpu.CompilerParams(vmem_limit_bytes=limit),
        cost_estimate=pl.CostEstimate(flops=cost, bytes_accessed=moved, transcendentals=0),
    )(*args, *after)


SENT = ((1, 0), (2, 0), (3, 1), (2, 1))
KEPT = ((0, 0), (3, 0), (0, 1), (1, 1))


def fetch(here_ref, a_ref, held, sems, first, parts):
    order = SENT + KEPT
    rows = held.shape[0] // (len(parts) * len(order))
    copies = []
    for own, stream in parts:
        base = (here_ref[2] if own else 1 - here_ref[2]) * 16 + stream * 2
        for owner, part in order:
            start = (base + lax.bitwise_xor(here_ref[0], owner) * 4 + part) * rows
            to = held.at[pl.ds(rows * len(copies), rows), :]
            block = a_ref.at[pl.ds(pl.multiple_of(start, rows), rows), :]
            copies.append(pltpu.make_async_copy(block, to, sems.at[first + len(copies)]))
    for copy in copies:
        copy.start()
    return copies


def multiply(a_ref, b_ref, out_ref, at):
    rows = a_ref.shape[0] // 3
    out_ref[...] = jnp.dot(a_ref[at * rows : (at + 1) * rows, :], b_ref[...], preferred_element_type=F32)


def pack(ref, value):
    rows = value.shape[0]
    top = jnp.maximum(jnp.max(jnp.abs(value), axis=0, keepdims=True), 1e-30)
    level = jnp.clip(jnp.ceil(jnp.log2(top * (1.0 / 32000.0)) * 256.0), -32000.0, 32000.0)
    scaled = value * jnp.exp2(level * (-1.0 / 256.0))
    ref[:rows, :] = jnp.round(scaled).astype(jnp.int32).astype(I16)
    ref[rows:, :] = jnp.broadcast_to(level, (TAIL, value.shape[1])).astype(jnp.int32).astype(I16)


def unpack(ref):
    rows = ref.shape[0] - TAIL
    level = ref[rows:, :].astype(jnp.int32).astype(F32)[0:1, :]
    return ref[:rows, :].astype(jnp.int32).astype(F32) * jnp.exp2(level * (1.0 / 256.0))


def first_messages(own_ref, other_ref, kept_ref, a_ref, b_ref):
    rows = own_ref.shape[0] // 4
    pack(a_ref, own_ref[:rows, :] + other_ref[:rows, :])
    pack(b_ref, own_ref[rows : 2 * rows, :] + other_ref[rows : 2 * rows, :])
    kept_ref[...] = own_ref[2 * rows :, :] + other_ref[2 * rows : 4 * rows, :]


def second_messages(sum_ref, a_in, b_in, kept_ref, a_ref, b_ref):
    rows = sum_ref.shape[0] // 4
    for part, (came, out) in enumerate(((a_in, a_ref), (b_in, b_ref))):
        at = 2 * part * rows
        total = sum_ref[at : at + 2 * rows, :] + unpack(came)
        kept_ref[part * rows : (part + 1) * rows, :] = total[:rows, :]
        pack(out, total[rows:, :])


def split_four(mine, work_ref, own_ref, message_refs, masks):
    quarter = work_ref.shape[0] // 4

    def rows_of(owner):
        return work_ref[pl.ds(pl.multiple_of(owner * quarter, quarter), quarter), :]

    for mask, out in zip(masks, message_refs):
        pack(out, rows_of(lax.bitwise_xor(mine, mask)))
    own_ref[...] = rows_of(mine)


def third_messages(here_ref, kept_ref, a_in, b_in, own_ref, m1_ref, m2_ref, m3_ref, work_ref):
    half = kept_ref.shape[0] // 2
    work_ref[:half, :] = kept_ref[:half, :] + unpack(a_in)
    work_ref[half:, :] = kept_ref[half:, :] + unpack(b_in)
    split_four(here_ref[1], work_ref, own_ref, (m1_ref, m2_ref, m3_ref), Z_ORDER)


def last_sum(own_ref, m1_in, m2_in, m3_in, out_ref):
    out_ref[...] = (own_ref[...] + unpack(m1_in) + unpack(m2_in) + unpack(m3_in)).astype(BF16)


def join(p0_ref, p1_ref, p2_ref, p3_ref, out_ref):
    rows = p0_ref.shape[0]
    for i, ref in enumerate((p0_ref, p1_ref, p2_ref, p3_ref)):
        out_ref[rows * i : rows * (i + 1), :] = ref[...]


def gram_messages(here_ref, mine_ref, came_ref, w_ref, other_ref, own_ref, m1_ref, m2_ref, m3_ref, work_ref):
    work_ref[...] = mine_ref[...] + came_ref[...] + gram_terms(here_ref, other_ref, (1, 2, 1), [w_ref])[0]
    split_four(here_ref[3] // 2, work_ref, own_ref, (m1_ref, m2_ref, m3_ref), Y_ORDER)


def gram_halves(here_ref, own_ref, m1_in, m2_in, m3_in, kept_ref, out_ref, work_ref):
    rows = kept_ref.shape[0]
    work_ref[...] = own_ref[...] + unpack(m1_in) + unpack(m2_in) + unpack(m3_in)
    half = here_ref[3] % 2
    kept_ref[...] = work_ref[pl.ds(pl.multiple_of(half * rows, rows), rows), :]
    pack(out_ref, work_ref[pl.ds(pl.multiple_of((1 - half) * rows, rows), rows), :])


def weights_kernel(here_ref, val_table, freq_ref, other_ref, ci_ref, vi_ref, ce_ref, *out_refs):
    shape = ci_ref.shape
    half = shape[1] // 2
    index = ci_ref[...]
    high, low = index // 128, index % 128
    cond = jnp.zeros(shape, F32)
    for row in range(ce_ref.shape[0]):
        table = jnp.broadcast_to(ce_ref[row : row + 1, :], shape)
        cond = jnp.where(high == row, jnp.take_along_axis(table, low, axis=1), cond)
    level = vi_ref[...]
    val = jnp.zeros(shape, F32)
    for row in range(val_table.shape[0]):
        val = jnp.where(level == row, val_table[row], val)
    spacing = cond - val
    swapped = jnp.concatenate([spacing[:, half:], spacing[:, :half]], axis=1)
    spacing = jnp.where(here_ref[1] % 2 == 1, swapped, spacing)
    for freq, out_ref in zip((freq_ref[0], other_ref[0:1, 0:1]), out_refs):
        out_ref[...] = 2.0 * spacing / (spacing * spacing + freq * freq)


def gram_terms(here_ref, ref, place, w_refs):
    stream, owner, core = place
    first = (lax.bitwise_xor(here_ref[2], core) * 4 + lax.bitwise_xor(here_ref[0], owner)) * 4 + stream * 2
    parts = [[] for _ in w_refs]
    for j in range(2):
        rows = ref[128 * j : 128 * (j + 1), :].astype(F32).T
        for part, w_ref in zip(parts, w_refs):
            w = w_ref[pl.ds(first + lax.bitwise_xor(here_ref[1] // 2, j), 1), :]
            part.append((rows * w).astype(BF16))
    return [jnp.dot(jnp.concatenate(part, axis=1), ref[...], preferred_element_type=F32) for part in parts]


def gram_step(here, weights, pieces, places, grams, extra=0):
    width = pieces[0].shape[1]
    count, kinds = len(pieces), len(weights)

    def body(here_ref, *refs):
        w_refs, came, before, out_refs = refs[:kinds], refs[kinds : kinds + count], refs[kinds + count : -kinds], refs[-kinds:]
        totals = [ref[...] for ref in before] or [None] * kinds
        for ref, place in zip(came, places):
            for kind, term in enumerate(gram_terms(here_ref, ref, place, w_refs)):
                totals[kind] = term if totals[kind] is None else totals[kind] + term
        for out_ref, total in zip(out_refs, totals):
            out_ref[...] = total

    return call(
        body,
        [((width, width), F32)] * kinds,
        here,
        *weights,
        *pieces,
        *grams,
        cost=2 * kinds * width * width * sum(p.shape[0] for p in pieces) + extra,
        specs=[SMEM] + [VMEM] * (kinds + count + len(grams)),
    )


def on_device(pair_elements, subspace, val_energy, cond_energy, val_index, cond_index, frequencies):
    here = jnp.stack([lax.axis_index(name).astype(jnp.int32) for name in PW + ("pair",)])
    rows, width = pair_elements.shape[0], subspace.shape[1]
    unit = rows // 64
    message = lambda count: ((count + TAIL, width), I16)
    sums = lambda count: ((count, width), F32)
    both = range(2)

    def first_other(here_ref, freq_ref, a_ref, b_ref, out_ref, held_ref, work_ref, sems):
        now = fetch(here_ref, a_ref, work_ref, sems, 0, [(False, 0)])
        later = fetch(here_ref, a_ref, held_ref, sems, 8, [(True, 0), (False, 1), (True, 1)])
        out_ref[16 * unit :, :] = jnp.full((8, width), freq_ref[0], F32)
        for copy in now:
            copy.wait()
        out_ref[: 16 * unit, :] = jnp.dot(work_ref[...], b_ref[...], preferred_element_type=F32)
        for copy in later:
            copy.wait()

    def first_own(a_ref, b_ref, own_ref, other_ref):
        multiply(a_ref, b_ref, own_ref, 0)
        multiply(a_ref, b_ref, other_ref, 1)

    def second_own(a_ref, b_ref, own_ref):
        multiply(a_ref, b_ref, own_ref, 2)

    kept, a, b = [None] * 2, [None] * 2, [None] * 2
    first = [sums(8 * unit)] + [message(4 * unit)] * 2
    depth = pair_elements.shape[1]
    cost = 2 * 16 * unit * depth * width
    other, held, done = call(
        first_other,
        [sums(16 * unit + 8), ((48 * unit, depth), BF16)],
        here,
        frequencies,
        pair_elements,
        subspace,
        specs=[SMEM, SMEM, ANY, VMEM],
        flag=True,
        cost=cost,
        scratch=[pltpu.VMEM((16 * unit, depth), BF16), pltpu.SemaphoreType.DMA((32,))],
        limit=VMEM_LARGE,
    )
    other_in = xor_permute(other, "pw_c", 1)
    own, other = call(first_own, [sums(16 * unit)] * 2, held, subspace, after=[done], cost=2 * cost)
    other, other_in = lax.optimization_barrier((other, other_in))
    kept[0], a[0], b[0], done = call(first_messages, first, own, other_in, flag=True)
    own = call(second_own, [sums(16 * unit)], held, subspace, after=[done], cost=cost)[0]
    kept[1], a[1], b[1] = call(first_messages, first, own, xor_permute(other, "pw_c", 1))

    last = None
    for s in both:
        a[s], b[s] = xor_permute(a[s], "pw_x", 1), xor_permute(b[s], "pw_x", 3)
    for s in both:
        after = [] if last is None else [last]
        kept[s], a[s], b[s], last = call(
            second_messages, [sums(4 * unit)] + [message(2 * unit)] * 2, kept[s], a[s], b[s], after=after, flag=True
        )
        a[s], b[s] = xor_permute(a[s], "pw_x", 3), xor_permute(b[s], "pw_x", 1)
    came = [None] * 2
    for s in both:
        own, *out, last = call(
            third_messages,
            [sums(unit)] + [message(unit)] * 3,
            here,
            kept[s],
            a[s],
            b[s],
            specs=[SMEM] + [VMEM] * 3,
            after=[last],
            flag=True,
            scratch=[pltpu.VMEM((4 * unit, width), F32)],
        )
        came[s] = [own] + [xor_permute(value, "pw_z", mask) for mask, value in zip(Z_ORDER, out)]
    weights = call(
        weights_kernel,
        [((rows // 128, 128), F32)] * 2,
        here,
        val_energy,
        frequencies,
        other_in[16 * unit :, :128],
        cond_index.reshape(-1, 128),
        val_index.reshape(-1, 128),
        cond_energy.reshape(-1, 128),
        specs=[SMEM] * 3 + [VMEM] * 4,
        after=[last],
    )

    last = weights[0]
    pieces = [None] * 2
    for s in both:
        own, last = call(last_sum, [((unit, width), BF16)], *came[s], after=[last], flag=True)
        pieces[s] = [own] + [xor_permute(own, "pw_z", mask) for mask in (1, 2, 3)]
    quarters, near, far = [None] * 2, [None] * 2, [None] * 2
    last = [last]
    for s in both:
        quarters[s], *last = call(join, [((4 * unit, width), BF16)], *pieces[s], after=last, flag=s == 0)
        near[s], far[s] = xor_permute(quarters[s], "pw_x", 1), xor_permute(quarters[s], "pw_x", 3)
        near[s], far[s] = lax.optimization_barrier((near[s], far[s]))
    grams = gram_step(here, weights, quarters, [(0, 0, 0), (1, 0, 0)], [], 3_000_000_000)
    near[0], far[0], grams = lax.optimization_barrier((near[0], far[0], grams))
    across = [xor_permute(far[0], "pw_x", 1), xor_permute(near[1], "pw_x", 3)]
    grams = gram_step(here, weights, [near[0], far[0]], [(0, 1, 0), (0, 3, 0)], grams)
    grams = gram_step(here, weights, [near[1], far[1], across[0]], [(1, 1, 0), (1, 3, 0), (0, 2, 0)], grams)
    mine, theirs = grams
    theirs, last = lax.optimization_barrier((theirs, across[1]))
    other = xor_permute(last, "pw_c", 1)
    theirs = xor_permute(theirs, "pw_c", 1)
    mine = gram_step(here, weights[:1], [last], [(1, 2, 0)], [mine])[0]

    part = width // 4
    own, *out = call(
        gram_messages,
        [sums(part)] + [message(part)] * 3,
        here,
        mine,
        theirs,
        weights[0],
        other,
        specs=[SMEM] + [VMEM] * 4,
        scratch=[pltpu.VMEM((width, width), F32)],
    )
    came = [xor_permute(value, "pair", 2 * mask) for mask, value in zip(Y_ORDER, out)]
    own, out = call(
        gram_halves,
        [sums(part // 2), message(part // 2)],
        here,
        own,
        *came,
        specs=[SMEM] + [VMEM] * 4,
        scratch=[pltpu.VMEM((part, width), F32)],
    )
    factor = -4.0 / (rows * lax.axis_size("pair"))

    def finish(own_ref, came_ref, out_ref):
        out_ref[...] = (own_ref[...] + unpack(came_ref)) * factor

    return call(finish, [sums(part // 2)], own, xor_permute(out, "pair", 1))[0][None]


def solution(mesh):
    torus = Mesh(mesh.devices.reshape(mesh.shape["pair"], 4, 4, 2), ("pair",) + PW)
    return jax.shard_map(
        on_device,
        mesh=torus,
        in_specs=(P("pair", PW), P(PW, None), P(), P(), P("pair"), P("pair"), P(PW)),
        out_specs=P(PW, "pair", None),
        check_vma=False,
    )
```

```python
import jax
import jax.numpy as jnp
from jax import lax
from jax.experimental import pallas as pl
from jax.experimental.pallas import tpu as pltpu
from jax.sharding import Mesh
from jax.sharding import PartitionSpec as P

PW = ("pw_x", "pw_z", "pw_c")
F32, BF16, I16 = jnp.float32, jnp.bfloat16, jnp.int16
TAIL = 16
Z_ORDER, Y_ORDER = (3, 2, 1), (2, 3, 1)
VMEM_LIMIT, VMEM_LARGE = 24 * 1024 * 1024, 40 * 1024 * 1024
SMEM, VMEM = pl.BlockSpec(memory_space=pltpu.SMEM), pl.BlockSpec(memory_space=pltpu.VMEM)
ANY = pl.BlockSpec(memory_space=pl.ANY)


def xor_permute(value, axis, mask):
    count = lax.axis_size(axis)
    return lax.ppermute(value, axis, [(i, i ^ mask) for i in range(count)])


def call(body, outs, *args, specs=None, after=(), flag=False, cost=0, scratch=(), limit=VMEM_LIMIT):
    specs = specs or [VMEM] * len(args)
    moved = sum(a.size * a.dtype.itemsize for a in args)
    outs = list(outs) + [((8, 128), F32)] * flag

    def kernel(*refs):
        refs = list(refs[: len(args)] + refs[len(args) + len(after) :])
        if flag:
            ref = refs.pop(len(args) + len(outs) - 1)
            ref[...] = jnp.zeros(ref.shape, F32)
        body(*refs)

    return pl.pallas_call(
        kernel,
        out_shape=[jax.ShapeDtypeStruct(shape, dtype) for shape, dtype in outs],
        in_specs=specs + [VMEM] * len(after),
        out_specs=[VMEM] * len(outs),
        scratch_shapes=list(scratch),
        compiler_params=pltpu.CompilerParams(vmem_limit_bytes=limit),
        cost_estimate=pl.CostEstimate(flops=cost, bytes_accessed=moved, transcendentals=0),
    )(*args, *after)


SENT = ((1, 0), (2, 0), (3, 1), (2, 1))
KEPT = ((0, 0), (3, 0), (0, 1), (1, 1))


def fetch(here_ref, a_ref, held, sems, first, parts):
    order = SENT + KEPT
    rows = held.shape[0] // (len(parts) * len(order))
    copies = []
    for own, stream in parts:
        base = (here_ref[2] if own else 1 - here_ref[2]) * 16 + stream * 2
        for owner, part in order:
            start = (base + lax.bitwise_xor(here_ref[0], owner) * 4 + part) * rows
            to = held.at[pl.ds(rows * len(copies), rows), :]
            block = a_ref.at[pl.ds(pl.multiple_of(start, rows), rows), :]
            copies.append(pltpu.make_async_copy(block, to, sems.at[first + len(copies)]))
    for copy in copies:
        copy.start()
    return copies


def multiply(a_ref, b_ref, out_ref, at):
    rows = a_ref.shape[0] // 3
    out_ref[...] = jnp.dot(a_ref[at * rows : (at + 1) * rows, :], b_ref[...], preferred_element_type=F32)


def pack(ref, value):
    rows = value.shape[0]
    top = jnp.maximum(jnp.max(jnp.abs(value), axis=0, keepdims=True), 1e-30)
    level = jnp.clip(jnp.ceil(jnp.log2(top * (1.0 / 32000.0)) * 256.0), -32000.0, 32000.0)
    scaled = value * jnp.exp2(level * (-1.0 / 256.0))
    ref[:rows, :] = jnp.round(scaled).astype(jnp.int32).astype(I16)
    ref[rows:, :] = jnp.broadcast_to(level, (TAIL, value.shape[1])).astype(jnp.int32).astype(I16)


def unpack(ref):
    rows = ref.shape[0] - TAIL
    level = ref[rows:, :].astype(jnp.int32).astype(F32)[0:1, :]
    return ref[:rows, :].astype(jnp.int32).astype(F32) * jnp.exp2(level * (1.0 / 256.0))


def first_messages(own_ref, other_ref, kept_ref, a_ref, b_ref):
    rows = own_ref.shape[0] // 4
    pack(a_ref, own_ref[:rows, :] + other_ref[:rows, :])
    pack(b_ref, own_ref[rows : 2 * rows, :] + other_ref[rows : 2 * rows, :])
    kept_ref[...] = own_ref[2 * rows :, :] + other_ref[2 * rows : 4 * rows, :]


def second_messages(sum_ref, a_in, b_in, kept_ref, a_ref, b_ref):
    rows = sum_ref.shape[0] // 4
    for part, (came, out) in enumerate(((a_in, a_ref), (b_in, b_ref))):
        at = 2 * part * rows
        total = sum_ref[at : at + 2 * rows, :] + unpack(came)
        kept_ref[part * rows : (part + 1) * rows, :] = total[:rows, :]
        pack(out, total[rows:, :])


def split_four(mine, work_ref, own_ref, message_refs, masks):
    quarter = work_ref.shape[0] // 4

    def rows_of(owner):
        return work_ref[pl.ds(pl.multiple_of(owner * quarter, quarter), quarter), :]

    for mask, out in zip(masks, message_refs):
        pack(out, rows_of(lax.bitwise_xor(mine, mask)))
    own_ref[...] = rows_of(mine)


def third_messages(here_ref, kept_ref, a_in, b_in, own_ref, m1_ref, m2_ref, m3_ref, work_ref):
    half = kept_ref.shape[0] // 2
    work_ref[:half, :] = kept_ref[:half, :] + unpack(a_in)
    work_ref[half:, :] = kept_ref[half:, :] + unpack(b_in)
    split_four(here_ref[1], work_ref, own_ref, (m1_ref, m2_ref, m3_ref), Z_ORDER)


def last_sum(own_ref, m1_in, m2_in, m3_in, out_ref):
    out_ref[...] = (own_ref[...] + unpack(m1_in) + unpack(m2_in) + unpack(m3_in)).astype(BF16)


def join(p0_ref, p1_ref, p2_ref, p3_ref, out_ref):
    rows = p0_ref.shape[0]
    for i, ref in enumerate((p0_ref, p1_ref, p2_ref, p3_ref)):
        out_ref[rows * i : rows * (i + 1), :] = ref[...]


def gram_messages(here_ref, mine_ref, came_ref, w_ref, other_ref, own_ref, m1_ref, m2_ref, m3_ref, work_ref):
    work_ref[...] = mine_ref[...] + came_ref[...] + gram_terms(here_ref, other_ref, (1, 2, 1), [w_ref])[0]
    split_four(here_ref[3] // 2, work_ref, own_ref, (m1_ref, m2_ref, m3_ref), Y_ORDER)


def gram_halves(here_ref, own_ref, m1_in, m2_in, m3_in, kept_ref, out_ref, work_ref):
    rows = kept_ref.shape[0]
    work_ref[...] = own_ref[...] + unpack(m1_in) + unpack(m2_in) + unpack(m3_in)
    half = here_ref[3] % 2
    kept_ref[...] = work_ref[pl.ds(pl.multiple_of(half * rows, rows), rows), :]
    pack(out_ref, work_ref[pl.ds(pl.multiple_of((1 - half) * rows, rows), rows), :])


def weights_kernel(here_ref, val_table, freq_ref, other_ref, ci_ref, vi_ref, ce_ref, *out_refs):
    shape = ci_ref.shape
    half = shape[1] // 2
    index = ci_ref[...]
    high, low = index // 128, index % 128
    cond = jnp.zeros(shape, F32)
    for row in range(ce_ref.shape[0]):
        table = jnp.broadcast_to(ce_ref[row : row + 1, :], shape)
        cond = jnp.where(high == row, jnp.take_along_axis(table, low, axis=1), cond)
    level = vi_ref[...]
    val = jnp.zeros(shape, F32)
    for row in range(val_table.shape[0]):
        val = jnp.where(level == row, val_table[row], val)
    spacing = cond - val
    swapped = jnp.concatenate([spacing[:, half:], spacing[:, :half]], axis=1)
    spacing = jnp.where(here_ref[1] % 2 == 1, swapped, spacing)
    for freq, out_ref in zip((freq_ref[0], other_ref[0:1, 0:1]), out_refs):
        out_ref[...] = 2.0 * spacing / (spacing * spacing + freq * freq)


def gram_terms(here_ref, ref, place, w_refs):
    stream, owner, core = place
    first = (lax.bitwise_xor(here_ref[2], core) * 4 + lax.bitwise_xor(here_ref[0], owner)) * 4 + stream * 2
    parts = [[] for _ in w_refs]
    for j in range(2):
        rows = ref[128 * j : 128 * (j + 1), :].astype(F32).T
        for part, w_ref in zip(parts, w_refs):
            w = w_ref[pl.ds(first + lax.bitwise_xor(here_ref[1] // 2, j), 1), :]
            part.append((rows * w).astype(BF16))
    return [jnp.dot(jnp.concatenate(part, axis=1), ref[...], preferred_element_type=F32) for part in parts]


def gram_step(here, weights, pieces, places, grams, extra=0):
    width = pieces[0].shape[1]
    count, kinds = len(pieces), len(weights)

    def body(here_ref, *refs):
        w_refs, came, before, out_refs = refs[:kinds], refs[kinds : kinds + count], refs[kinds + count : -kinds], refs[-kinds:]
        totals = [ref[...] for ref in before] or [None] * kinds
        for ref, place in zip(came, places):
            for kind, term in enumerate(gram_terms(here_ref, ref, place, w_refs)):
                totals[kind] = term if totals[kind] is None else totals[kind] + term
        for out_ref, total in zip(out_refs, totals):
            out_ref[...] = total

    return call(
        body,
        [((width, width), F32)] * kinds,
        here,
        *weights,
        *pieces,
        *grams,
        cost=2 * kinds * width * width * sum(p.shape[0] for p in pieces) + extra,
        specs=[SMEM] + [VMEM] * (kinds + count + len(grams)),
    )


def on_device(pair_elements, subspace, val_energy, cond_energy, val_index, cond_index, frequencies):
    here = jnp.stack([lax.axis_index(name).astype(jnp.int32) for name in PW + ("pair",)])
    rows, width = pair_elements.shape[0], subspace.shape[1]
    unit = rows // 64
    message = lambda count: ((count + TAIL, width), I16)
    sums = lambda count: ((count, width), F32)
    both = range(2)

    def first_other(here_ref, freq_ref, a_ref, b_ref, out_ref, held_ref, work_ref, sems):
        now = fetch(here_ref, a_ref, work_ref, sems, 0, [(False, 0)])
        later = fetch(here_ref, a_ref, held_ref, sems, 8, [(True, 0), (False, 1), (True, 1)])
        out_ref[16 * unit :, :] = jnp.full((8, width), freq_ref[0], F32)
        for copy in now:
            copy.wait()
        out_ref[: 16 * unit, :] = jnp.dot(work_ref[...], b_ref[...], preferred_element_type=F32)
        for copy in later:
            copy.wait()

    def first_own(a_ref, b_ref, own_ref, other_ref):
        multiply(a_ref, b_ref, own_ref, 0)
        multiply(a_ref, b_ref, other_ref, 1)

    def second_own(a_ref, b_ref, own_ref):
        multiply(a_ref, b_ref, own_ref, 2)

    kept, a, b = [None] * 2, [None] * 2, [None] * 2
    first = [sums(8 * unit)] + [message(4 * unit)] * 2
    depth = pair_elements.shape[1]
    cost = 2 * 16 * unit * depth * width
    other, held, done = call(
        first_other,
        [sums(16 * unit + 8), ((48 * unit, depth), BF16)],
        here,
        frequencies,
        pair_elements,
        subspace,
        specs=[SMEM, SMEM, ANY, VMEM],
        flag=True,
        cost=cost,
        scratch=[pltpu.VMEM((16 * unit, depth), BF16), pltpu.SemaphoreType.DMA((32,))],
        limit=VMEM_LARGE,
    )
    other_in = xor_permute(other, "pw_c", 1)
    own, other = call(first_own, [sums(16 * unit)] * 2, held, subspace, after=[done], cost=2 * cost)
    other, other_in = lax.optimization_barrier((other, other_in))
    kept[0], a[0], b[0], done = call(first_messages, first, own, other_in, flag=True)
    own = call(second_own, [sums(16 * unit)], held, subspace, after=[done], cost=cost)[0]
    kept[1], a[1], b[1] = call(first_messages, first, own, xor_permute(other, "pw_c", 1))

    last = None
    for s in both:
        a[s], b[s] = xor_permute(a[s], "pw_x", 1), xor_permute(b[s], "pw_x", 3)
    for s in both:
        after = [] if last is None else [last]
        kept[s], a[s], b[s], last = call(
            second_messages, [sums(4 * unit)] + [message(2 * unit)] * 2, kept[s], a[s], b[s], after=after, flag=True
        )
        a[s], b[s] = xor_permute(a[s], "pw_x", 3), xor_permute(b[s], "pw_x", 1)
    came = [None] * 2
    for s in both:
        own, *out, last = call(
            third_messages,
            [sums(unit)] + [message(unit)] * 3,
            here,
            kept[s],
            a[s],
            b[s],
            specs=[SMEM] + [VMEM] * 3,
            after=[last],
            flag=True,
            scratch=[pltpu.VMEM((4 * unit, width), F32)],
        )
        came[s] = [own] + [xor_permute(value, "pw_z", mask) for mask, value in zip(Z_ORDER, out)]
    weights = call(
        weights_kernel,
        [((rows // 128, 128), F32)] * 2,
        here,
        val_energy,
        frequencies,
        other_in[16 * unit :, :128],
        cond_index.reshape(-1, 128),
        val_index.reshape(-1, 128),
        cond_energy.reshape(-1, 128),
        specs=[SMEM] * 3 + [VMEM] * 4,
        after=[last],
    )

    last = weights[0]
    pieces = [None] * 2
    for s in both:
        own, last = call(last_sum, [((unit, width), BF16)], *came[s], after=[last], flag=True)
        pieces[s] = [own] + [xor_permute(own, "pw_z", mask) for mask in (1, 2, 3)]
    quarters, near, far = [None] * 2, [None] * 2, [None] * 2
    last = [last]
    for s in both:
        quarters[s], *last = call(join, [((4 * unit, width), BF16)], *pieces[s], after=last, flag=s == 0)
        near[s], far[s] = xor_permute(quarters[s], "pw_x", 1), xor_permute(quarters[s], "pw_x", 3)
        near[s], far[s] = lax.optimization_barrier((near[s], far[s]))
    grams = gram_step(here, weights, quarters, [(0, 0, 0), (1, 0, 0)], [], 3_000_000_000)
    near[0], far[0], grams = lax.optimization_barrier((near[0], far[0], grams))
    across = [xor_permute(far[0], "pw_x", 1), xor_permute(near[1], "pw_x", 3)]
    grams = gram_step(here, weights, [near[0], far[0]], [(0, 1, 0), (0, 3, 0)], grams)
    grams = gram_step(here, weights, [near[1], far[1], across[0]], [(1, 1, 0), (1, 3, 0), (0, 2, 0)], grams)
    mine, theirs = grams
    other = xor_permute(across[1], "pw_c", 1)
    theirs = xor_permute(theirs, "pw_c", 1)
    mine = gram_step(here, weights[:1], [across[1]], [(1, 2, 0)], [mine], 9_000_000_000)[0]

    part = width // 4
    own, *out = call(
        gram_messages,
        [sums(part)] + [message(part)] * 3,
        here,
        mine,
        theirs,
        weights[0],
        other,
        specs=[SMEM] + [VMEM] * 4,
        cost=0,
        scratch=[pltpu.VMEM((width, width), F32)],
    )
    came = [xor_permute(value, "pair", 2 * mask) for mask, value in zip(Y_ORDER, out)]
    own, out = call(
        gram_halves,
        [sums(part // 2), message(part // 2)],
        here,
        own,
        *came,
        specs=[SMEM] + [VMEM] * 4,
        scratch=[pltpu.VMEM((part, width), F32)],
    )
    factor = -4.0 / (rows * lax.axis_size("pair"))

    def finish(own_ref, came_ref, out_ref):
        out_ref[...] = (own_ref[...] + unpack(came_ref)) * factor

    return call(finish, [sums(part // 2)], own, xor_permute(out, "pair", 1))[0][None]


def solution(mesh):
    torus = Mesh(mesh.devices.reshape(mesh.shape["pair"], 4, 4, 2), ("pair",) + PW)
    return jax.shard_map(
        on_device,
        mesh=torus,
        in_specs=(P("pair", PW), P(PW, None), P(), P(), P("pair"), P("pair"), P(PW)),
        out_specs=P(PW, "pair", None),
        check_vma=False,
    )
```
